32 devices in a mesh: seq: 4 (over x, core), rows: 8 (over z, y).
Axes of the slice: x: 2, y: 2, z: 4, core: 2. Of those that a mesh axis runs over, the one named last changes fastest.
Arguments:
- blocks: bfloat16 [32, 1024, 768], P('rows', 'seq'), may hold values from -6 to 6
- segment_ids: int32 [32, 1024], P('rows', 'seq'), may hold values from 0 to 129, as said below
- cotangent: bfloat16 [32, 1024, 768], P('rows', 'seq'), may hold values from -6 to 6
- w_query: bfloat16 [768, 768], replicated, may hold values from -0.3125 to 0.3125
- w_key: bfloat16 [768, 768], replicated, may hold values from -0.3125 to 0.3125
- w_value: bfloat16 [768, 768], replicated, may hold values from -0.21875 to 0.21875
- w_out: bfloat16 [768, 768], replicated, may hold values from -0.625 to 0.625
- norm_one: float32 [768], replicated, may hold values from 0.1 to 1.9
- norm_two: float32 [768], replicated, may hold values from 0.1 to 1.9
- w_gate: bfloat16 [768, 2048], replicated, may hold values from -0.21875 to 0.21875
- w_up: bfloat16 [768, 2048], replicated, may hold values from -0.21875 to 0.21875
- w_down: bfloat16 [2048, 768], replicated, may hold values from -0.125 to 0.125
Outputs:
- output: bfloat16 [32, 1024, 768], P('rows', 'seq')
- d_blocks: bfloat16 [32, 1024, 768], P('rows', 'seq')
- d_w_query: float32 [768, 768], replicated
- d_w_key: float32 [768, 768], replicated
- d_w_value: float32 [768, 768], replicated
- d_w_out: float32 [768, 768], replicated
- d_norm_one: float32 [768], replicated
- d_norm_two: float32 [768], replicated
- d_w_gate: float32 [768, 2048], replicated
- d_w_up: float32 [768, 2048], replicated
- d_w_down: float32 [2048, 768], replicated
The draws below stay inside these ranges and needn't reach their ends.
Inputs may be any that keep to these rules, and one draw needn't show every extreme that they name: `segment_ids`: ids never fall along a row and each row begins with 0; equal ids in a row mark one document, and the segments after a row's longest document are short documents and padding. In every row one document has its first block at an index from 1 to 128 and its last block at an index from 895 to 1024 - 2 (block indices counted from 0).
All inputs are finite; a program needn't handle non-finite values.
Results may differ from the reference program's by a relative error of at most 0.019.
Values may be sent and summed in bfloat16 or wider, within the bound.
A program may use at most 384 MiB of HBM per device.

```python
import math
import jax
import jax.numpy as jnp
from jax import lax

D = 768
HEADS = 12
HEAD_DIM = 64
FF = 2048
L = 1024
SHARD = 256
ROWS = 32


def draw_segment_ids(key, part):
    key = jax.random.fold_in(key, 11)
    first_key, last_key, extra_key = jax.random.split(key, 3)
    begin = jax.random.randint(first_key, (ROWS, 1), 1, SHARD // 2 + 1)
    finish = jax.random.randint(last_key, (ROWS, 1), L - SHARD // 2, L)
    row_index = jnp.arange(ROWS, dtype=jnp.int32)[:, None]
    first_row = row_index == 0
    finish = jnp.where(first_row, L - SHARD // 2, finish).astype(jnp.int32)
    places = jnp.arange(L, dtype=jnp.int32)[None, :]
    extra = (jax.random.randint(extra_key, (ROWS, L), 0, 24) == 0) | first_row
    starts = (places == begin) | (places == finish) | extra & (places > finish)
    return jnp.cumsum(starts.astype(jnp.int32), axis=1).astype(jnp.int32)


def shard_levels(own_key, shape, pieces, least, top_value):
    factor_of, own = 1.0, jax.random.fold_in(own_key, 6)
    for position, parts in pieces:
        draws = jnp.exp(jax.random.uniform(jax.random.fold_in(own, position), (parts,), jnp.float32, least / len(pieces), top_value / len(pieces)))
        factor_of = factor_of * jnp.repeat(draws, shape[position] // parts).reshape([-1 if axis == position else 1 for axis in range(len(shape))])
    return factor_of


def gaussian(own_key, extent, spread, most, shards=(), kind=jnp.bfloat16):
    drawn = jax.random.normal(own_key, extent, jnp.float32) * spread
    if len(shards) > 0:
        drawn = shard_levels(own_key, extent, shards, -0.22, 0.18) * drawn
    return jnp.clip(drawn, min=-most, max=most).astype(kind)


def setup_inputs(seed: int = 0) -> dict:
    key_of = jax.random.split(jax.random.key(seed), 13)
    return {
        "blocks": gaussian(key_of[0], (ROWS, L, D), 1.0, 6.0, ((0, 8), (1, 4))),
        "segment_ids": draw_segment_ids(jax.random.fold_in(key_of[12], 71), 0),
        "cotangent": gaussian(key_of[2], (ROWS, L, D), 1.0, 6.0, ((0, 8), (1, 4))),
        "w_query": gaussian(key_of[3], (D, D), (D // 2) ** -0.5, 0.3125),
        "w_key": gaussian(key_of[4], (D, D), (D // 2) ** -0.5, 0.3125),
        "w_value": gaussian(key_of[5], (D, D), D ** -0.5, 0.21875),
        "w_out": gaussian(key_of[6], (D, D), (D // 8) ** -0.5, 0.625),
        "norm_one": jnp.clip(1.0 + 0.18 * jax.random.normal(key_of[7], (D,), jnp.float32), 0.1, 1.9),
        "norm_two": jnp.clip(1.0 + 0.18 * jax.random.normal(key_of[8], (D,), jnp.float32), 0.1, 1.9),
        "w_gate": gaussian(key_of[9], (D, FF), D ** -0.5, 0.21875),
        "w_up": gaussian(key_of[10], (D, FF), D ** -0.5, 0.21875),
        "w_down": gaussian(key_of[11], (FF, D), FF ** -0.5, 0.125),
    }


EPSILON = 1e-06
MASKED = -1000000000.0

@jax.custom_vjp
def low(v):
    return lax.optimization_barrier(v.astype(jnp.bfloat16)).astype(jnp.float32)

@jax.custom_vjp
def low_back(v):
    return v

def low_keep(v):
    return (low(v), None)

def low_pass(kept, grad):
    return (grad,)

def back_keep(v):
    return (v, None)

def back_low(kept, grad):
    return (low(grad),)
low.defvjp(low_keep, low_pass)
low_back.defvjp(back_keep, back_low)

def rms_norm(value, gain):
    return value * lax.rsqrt(lax.optimization_barrier(jnp.mean(value * value, axis=-1, keepdims=True)) + EPSILON) * gain

def forward(block_part, doc_ids, w_query, w_key, w_value, w_out, norm_one, norm_two, w_gate, w_up, w_down):
    group_rows, length, features = block_part.shape
    highest = lax.Precision.HIGHEST
    normed_one = low(rms_norm(block_part, norm_one))

    def project(weight):
        made = jnp.einsum('rld,de->rle', normed_one, weight, precision=highest)
        return low(low_back(made)).reshape(group_rows, length, HEADS, HEAD_DIM)
    query_part = project(w_query)
    key_part = project(w_key)
    value_part = project(w_value)
    scores = low_back(jnp.einsum('rqhd,rkhd->rhqk', query_part, key_part, precision=highest) * HEAD_DIM ** (-0.5))
    same_doc = doc_ids[:, None, :, None] == doc_ids[:, None, None, :]
    scores = jnp.where(same_doc, scores, MASKED)
    largest = lax.optimization_barrier(jnp.max(scores, axis=-1, keepdims=True))
    exponent = jnp.exp(scores - largest)
    probability = low(exponent / lax.optimization_barrier(jnp.sum(exponent, axis=-1, keepdims=True)))
    mixed_heads = jnp.einsum('rhqk,rkhd->rqhd', probability, value_part, precision=highest)
    mixed_heads = low(low_back(mixed_heads)).reshape(group_rows, length, features)
    x_one = block_part + low_back(jnp.einsum('rld,de->rle', mixed_heads, w_out, precision=highest))
    normed_two = low(rms_norm(x_one, norm_two))
    gate_value = low_back(jnp.einsum('rld,df->rlf', normed_two, w_gate, precision=highest))
    up_value = low_back(jnp.einsum('rld,df->rlf', normed_two, w_up, precision=highest))
    hidden = low(jax.nn.gelu(gate_value, approximate=True) * up_value)
    return x_one + low_back(jnp.einsum('rlf,fd->rld', hidden, w_down, precision=highest))

def reference(blocks, segment_ids, cotangent, w_query, w_key, w_value, w_out, norm_one, norm_two, w_gate, w_up, w_down):
    weights = tuple((w.astype(jnp.float32) for w in (w_query, w_key, w_value, w_out, norm_one, norm_two, w_gate, w_up, w_down)))
    group_rows = math.gcd(ROWS, max(1, 4096 // L))
    group_count = ROWS // group_rows
    block_groups = blocks.astype(jnp.float32).reshape(group_count, group_rows, L, D)
    id_groups = segment_ids.reshape(group_count, group_rows, L)
    grad_groups = cotangent.astype(jnp.float32).reshape(group_count, group_rows, L, D)

    def scan_step(totals, scan_item):
        block_part, doc_ids, grad_part = scan_item

        def apply(x_in, *params):
            return forward(x_in, doc_ids, *params)
        result, pullback = jax.vjp(apply, block_part, *weights)
        grads = pullback(grad_part)
        totals = tuple((t + g for t, g in zip(totals, grads[1:])))
        return (totals, (result.astype(jnp.bfloat16), grads[0].astype(jnp.bfloat16)))
    zero_grads = tuple((jnp.zeros_like(w) for w in weights))
    totals, (results, input_grads) = lax.scan(scan_step, zero_grads, (block_groups, id_groups, grad_groups))
    return (results.reshape(ROWS, L, D), input_grads.reshape(ROWS, L, D), totals[0], totals[1], totals[2], totals[3], totals[4], totals[5], totals[6], totals[7], totals[8])
```

```python
from functools import partial

import jax
import jax.numpy as jnp
from jax import lax
from jax.experimental import pallas as pl
from jax.experimental.pallas import tpu as pltpu
from jax.sharding import PartitionSpec as P

MESH = pl.DeviceIdType.MESH
HEAD_DIM = 64
EPSILON = 1e-06
MASKED = -1000000000.0
PIECE = 768
NT = 3
NC = 12


def flip(index, bit):
    unit = 1 << bit
    own = lax.rem(index // unit, 2)
    return own, index + (1 - 2 * own) * unit


class Links:
    def __init__(self, row_bits):
        seq, row = lax.axis_index("seq"), lax.axis_index("rows")
        self.core, other = flip(seq, 0)
        self.other_core = (other, row)
        x_bit, x_other = flip(seq, 1)
        dims = [(x_bit, (x_other, row))]
        for bit in range(row_bits):
            own, partner = flip(row, bit)
            dims.append((own, (seq, partner)))
        self.halving = dims[:3]
        self.extra = dims[3:]
        n = len(self.halving)
        orders = [(0, 1, 2), (1, 2, 0), (2, 0, 1)]
        self.orders = [[d for d in order if d < n] for order in orders]

    def all(self):
        return [self.other_core] + [p for _, p in self.halving + self.extra]


class Reducer:
    def __init__(self, links, grads, landing, small, send, recv, free):
        self.l, self.g, self.landing, self.small = links, grads, landing, small
        self.send, self.recv, self.free = send, recv, free
        n, e = len(links.halving), len(links.extra)
        self.n, self.e = n, e
        self.steps = 2 + 2 * n + e + 1

    def span(self, t, level):
        low = 0
        for k in range(level):
            low = low + self.l.halving[self.l.orders[t][k]][0] * (PIECE >> (k + 1))
        return low

    def copies(self, c, stage):
        l, n, e = self.l, self.n, self.e
        core = l.core
        if stage == 0:
            return [self.make(self.g.at[c, :, 1 - core], self.landing.at[c, :, pl.ds(0, PIECE)], c, stage, 0, l.other_core)]
        if stage <= n:
            out = []
            for t in range(NT):
                own, partner = l.halving[l.orders[t][stage - 1]]
                rows = PIECE >> stage
                low = pl.multiple_of(self.span(t, stage - 1) + (1 - own) * rows, 16)
                at = 2 * PIECE - 2 * rows
                out.append(self.make(self.g.at[c, t, core, pl.ds(low, rows)], self.landing.at[c, t, pl.ds(at, rows)], c, stage, t, partner))
            return out
        rows = PIECE >> n
        if stage <= n + e:
            partner = l.extra[stage - n - 1][1]
            out = []
            for t in range(NT):
                low = pl.multiple_of(self.span(t, n), 16)
                out.append(self.make(self.g.at[c, t, core, pl.ds(low, rows)], self.small.at[c, stage - n - 1, t], c, stage, t, partner))
            return out
        k = 2 * n + e + 1 - stage
        if k > 0:
            out = []
            for t in range(NT):
                partner = l.halving[l.orders[t][k - 1]][1]
                rows = PIECE >> k
                low = pl.multiple_of(self.span(t, k), 16)
                view = self.g.at[c, t, core, pl.ds(low, rows)]
                out.append(self.make(view, view, c, stage, t, partner))
            return out
        view = self.g.at[c, :, core]
        return [self.make(view, view, c, stage, 0, l.other_core)]

    def make(self, src, dst, c, stage, t, partner):
        return pltpu.make_async_remote_copy(
            src_ref=src, dst_ref=dst, send_sem=self.send.at[c, stage, t], recv_sem=self.recv.at[c, stage, t],
            device_id=partner, device_id_type=MESH)

    def fold(self, c, stage):
        n, e = self.n, self.e
        core = self.l.core
        if stage <= n:
            rows = PIECE >> stage
            at = 0 if stage == 0 else 2 * PIECE - 2 * rows
            for t in range(NT):
                low = pl.multiple_of(self.span(t, stage), 16)
                view = self.g.at[c, t, core, pl.ds(low, rows)]
                got = self.landing[c, t, pl.ds(at, rows)]
                view[...] = (view[...].astype(jnp.float32) + got.astype(jnp.float32)).astype(jnp.bfloat16)
        elif stage <= n + e:
            rows = PIECE >> n
            for t in range(NT):
                low = pl.multiple_of(self.span(t, n), 16)
                view = self.g.at[c, t, core, pl.ds(low, rows)]
                got = self.small[c, stage - n - 1, t]
                view[...] = (view[...].astype(jnp.float32) + got.astype(jnp.float32)).astype(jnp.bfloat16)

    def step(self, k, c):
        if k > 0:
            for copy in self.copies(c, k - 1):
                copy.wait()
            self.fold(c, k - 1)
            if k - 1 <= self.n:
                for t, partner in self.partners(k - 1):
                    pl.semaphore_signal(self.free.at[k - 1, t], inc=1, device_id=partner, device_id_type=MESH)
        if k < self.steps - 1:
            back = 2 * self.n + self.e + 1 - k
            if back <= self.n:
                for t, _ in self.partners(back):
                    pl.semaphore_wait(self.free.at[back, t], 1)
            for copy in self.copies(c, k):
                copy.start()

    def partners(self, level):
        if level == 0:
            return [(0, self.l.other_core)]
        return [(t, self.l.halving[self.l.orders[t][level - 1]][1]) for t in range(NT)]

    def round(self, r, finish):
        for k in reversed(range(self.steps)):
            c = r - k

            @pl.when((c >= 0) & (c < NC))
            def _():
                self.step(k, c)
                if k == self.steps - 1:
                    finish(c)


def scratch(row_bits):
    n, e = min(3, row_bits + 1), max(0, row_bits - 2)
    stages = 2 + 2 * n + e
    return [
        pltpu.VMEM((NC, NT, 2, PIECE, 128), jnp.bfloat16),
        pltpu.VMEM((NC, NT, 2 * PIECE - (PIECE >> n), 128), jnp.bfloat16),
        pltpu.VMEM((NC, max(e, 1), NT, PIECE >> n, 128), jnp.bfloat16),
        pltpu.SemaphoreType.DMA((NC, stages, NT)),
        pltpu.SemaphoreType.DMA((NC, stages, NT)),
        pltpu.SemaphoreType.REGULAR((n + 1, NT)),
    ]


def greet_row(count):
    seq, row = lax.axis_index("seq"), lax.axis_index("rows")
    barrier = pltpu.get_barrier_semaphore()
    for d in range(1, count):
        pl.semaphore_signal(barrier, inc=1, device_id=(lax.rem(seq + d, count), row), device_id_type=MESH)
    pl.semaphore_wait(barrier, count - 1)


def to_rows_kernel(count, blocks, ids, cotangent, x_out, ids_out, g_out, send, recv, own):
    seq, row = lax.axis_index("seq"), lax.axis_index("rows")
    greet_row(count)
    positions = blocks.shape[1]
    pairs = ((blocks, x_out, positions), (ids, ids_out, 8), (cotangent, g_out, positions))
    local, remote = [], []
    for a, (src, dst, size) in enumerate(pairs):
        mine = pl.ds(pl.multiple_of(seq * size, size), size)
        copy = pltpu.make_async_copy(src.at[seq], dst.at[mine], own.at[a])
        copy.start()
        local.append(copy)
        for d in range(1, count):
            peer = lax.rem(seq + d, count)
            copy = pltpu.make_async_remote_copy(
                src_ref=src.at[peer], dst_ref=dst.at[mine], send_sem=send.at[a, d], recv_sem=recv.at[a, d],
                device_id=(peer, row), device_id_type=MESH)
            copy.start()
            remote.append(copy)
    for copy in local + remote:
        copy.wait()


def to_rows(blocks, ids, cotangent):
    count, positions, features = blocks.shape
    anywhere = pl.BlockSpec(memory_space=pl.ANY)
    flat = jax.ShapeDtypeStruct((count * positions, features), blocks.dtype)
    wide = jnp.broadcast_to(ids[:, None, :], (count, 8, positions))
    return pl.pallas_call(
        partial(to_rows_kernel, count),
        out_shape=(flat, jax.ShapeDtypeStruct((count * 8, positions), ids.dtype), flat),
        in_specs=[anywhere] * 3, out_specs=[anywhere] * 3,
        scratch_shapes=[pltpu.SemaphoreType.DMA((3, count)), pltpu.SemaphoreType.DMA((3, count)), pltpu.SemaphoreType.DMA((3,))],
        compiler_params=pltpu.CompilerParams(collective_id=0, has_side_effects=True),
    )(blocks, wide, cotangent)


def sum_kernel(row_bits, count, src, y, dx, out, y_out, dx_out, grads, landing, small, send, recv, free, in_sem, out_sem, row_send, row_recv, own):
    links = Links(row_bits)
    seq, row = lax.axis_index("seq"), lax.axis_index("rows")
    reducer = Reducer(links, grads, landing, small, send, recv, free)
    barrier = pltpu.get_barrier_semaphore()
    for partner in links.all():
        pl.semaphore_signal(barrier, inc=1, device_id=partner, device_id_type=MESH)
    diagonal = (3 - seq, row)
    pl.semaphore_signal(barrier, inc=1, device_id=diagonal, device_id_type=MESH)
    pl.semaphore_wait(barrier, len(links.all()) + 1)

    def load(c):
        return pltpu.make_async_copy(src.at[c], grads.at[c], in_sem.at[c])

    def store(c):
        return pltpu.make_async_copy(grads.at[c], out.at[c], out_sem.at[c])

    for c in range(NC):
        load(c).start()
    moves = []
    positions = y.shape[0] // count
    for a, (a_src, a_dst) in enumerate(((y, y_out), (dx, dx_out))):
        copy = pltpu.make_async_copy(a_src.at[pl.ds(pl.multiple_of(seq * positions, positions), positions)], a_dst.at[seq], own.at[a])
        copy.start()
        moves.append(copy)
        for d in range(1, count):
            peer = lax.rem(seq + d, count)
            copy = pltpu.make_async_remote_copy(
                src_ref=a_src.at[pl.ds(pl.multiple_of(peer * positions, positions), positions)], dst_ref=a_dst.at[seq],
                send_sem=row_send.at[a, d], recv_sem=row_recv.at[a, d], device_id=(peer, row), device_id_type=MESH)
            copy.start()
            moves.append(copy)

    def body(r, _):
        @pl.when(r < NC)
        def _():
            load(r).wait()

        reducer.round(r, lambda c: store(c).start())
        return 0

    lax.fori_loop(0, NC + reducer.steps - 1, body, 0)
    for c in range(NC):
        store(c).wait()
    for copy in moves:
        copy.wait()


def sum_all(grads, y, dx, row_bits, count):
    anywhere = pl.BlockSpec(memory_space=pl.ANY)
    shape = (count, y.shape[0] // count, y.shape[1])
    back = jax.ShapeDtypeStruct(shape, y.dtype)
    return pl.pallas_call(
        partial(sum_kernel, row_bits, count),
        out_shape=(jax.ShapeDtypeStruct(grads.shape, grads.dtype), back, back),
        in_specs=[anywhere] * 3, out_specs=[anywhere] * 3,
        scratch_shapes=scratch(row_bits) + [pltpu.SemaphoreType.DMA((NC,)), pltpu.SemaphoreType.DMA((NC,)),
            pltpu.SemaphoreType.DMA((2, count)), pltpu.SemaphoreType.DMA((2, count)), pltpu.SemaphoreType.DMA((2,))],
        compiler_params=pltpu.CompilerParams(collective_id=1, has_side_effects=True, vmem_limit_bytes=60 * 2**20),
    )(grads, y, dx)


def rms_norm(value, gain):
    return value * lax.rsqrt(jnp.mean(value * value, axis=-1, keepdims=True) + EPSILON) * gain


def outer_sum(left, right):
    return lax.dot_general(left, right, (((0,), (0,)), ((), ())), preferred_element_type=jnp.float32)


def back_project(gradient, weight):
    return lax.dot_general(gradient, weight, (((1,), (1,)), ((), ())), preferred_element_type=jnp.float32)


def halves(piece):
    return piece.reshape(PIECE, 2, 128).transpose(1, 0, 2).astype(jnp.bfloat16)


def whole(pair):
    return pair.transpose(1, 0, 2).reshape(PIECE, 256)


def body(row_bits, blocks, segment_ids, cotangent, w_query, w_key, w_value, w_out, norm_one, norm_two, w_gate, w_up, w_down):
    count, positions, features = blocks.shape
    x_low, ids, grad_low = to_rows(blocks, segment_ids, cotangent)
    ids = ids.reshape(count, 8, positions)[:, 0, :].reshape(-1)
    tokens = x_low.shape[0]
    heads = features // HEAD_DIM
    x_flat = x_low.astype(jnp.float32)
    normed_one = rms_norm(x_flat, norm_one).astype(jnp.bfloat16)

    def project(weight):
        made = jnp.dot(normed_one, weight, preferred_element_type=jnp.float32)
        return made.astype(jnp.bfloat16).reshape(tokens, heads, HEAD_DIM)

    query, key, value = project(w_query), project(w_key), project(w_value)
    same_doc = ids[:, None] == ids[None, :]
    scores = jnp.einsum("qhd,khd->hqk", query, key, preferred_element_type=jnp.float32) * HEAD_DIM ** (-0.5)
    scores = jnp.where(same_doc, scores, MASKED)
    exponent = jnp.exp(scores - jnp.max(scores, axis=-1, keepdims=True))
    probability = (exponent / jnp.sum(exponent, axis=-1, keepdims=True)).astype(jnp.bfloat16)
    mixed = jnp.einsum("hqk,khd->qhd", probability, value, preferred_element_type=jnp.float32)
    mixed = mixed.astype(jnp.bfloat16).reshape(tokens, features)
    x_one = x_flat + jnp.dot(mixed, w_out, preferred_element_type=jnp.float32)
    normed_two = rms_norm(x_one, norm_two).astype(jnp.bfloat16)
    gate_value = jnp.dot(normed_two, w_gate, preferred_element_type=jnp.float32)
    up_value = jnp.dot(normed_two, w_up, preferred_element_type=jnp.float32)
    activated, gelu_back = jax.vjp(partial(jax.nn.gelu, approximate=True), gate_value)
    hidden = (activated * up_value).astype(jnp.bfloat16)
    result = (x_one + jnp.dot(hidden, w_down, preferred_element_type=jnp.float32)).astype(jnp.bfloat16)
    gradient = grad_low.astype(jnp.float32)
    d_down = outer_sum(hidden, grad_low)
    d_hidden = back_project(grad_low, w_down)
    d_gate = gelu_back(d_hidden * up_value)[0].astype(jnp.bfloat16)
    d_up = (d_hidden * activated).astype(jnp.bfloat16)
    d_gate_w = outer_sum(normed_two, d_gate)
    d_up_w = outer_sum(normed_two, d_up)
    d_normed_two = back_project(d_gate, w_gate) + back_project(d_up, w_up)
    d_x_part, d_norm_two = jax.vjp(rms_norm, x_one, norm_two)[1](d_normed_two)
    d_x_one = gradient + d_x_part
    d_branch = d_x_one.astype(jnp.bfloat16)
    d_out_w = outer_sum(mixed, d_branch)
    d_mixed = back_project(d_branch, w_out).astype(jnp.bfloat16).reshape(tokens, heads, HEAD_DIM)
    d_probs = jnp.einsum("qhd,khd->hqk", d_mixed, value, preferred_element_type=jnp.float32)
    wide = probability.astype(jnp.float32)
    d_scores = (wide * (d_probs - jnp.sum(wide * d_probs, axis=-1, keepdims=True))).astype(jnp.bfloat16)
    scale = HEAD_DIM ** (-0.5)
    d_query = jnp.einsum("hqk,khd->qhd", d_scores, key, preferred_element_type=jnp.float32) * scale
    d_key = jnp.einsum("hqk,qhd->khd", d_scores, query, preferred_element_type=jnp.float32) * scale
    d_value = jnp.einsum("hqk,qhd->khd", probability, d_mixed, preferred_element_type=jnp.float32)
    d_query, d_key, d_value = (d.astype(jnp.bfloat16).reshape(tokens, features) for d in (d_query, d_key, d_value))
    d_normed_one = back_project(d_query, w_query) + back_project(d_key, w_key) + back_project(d_value, w_value)
    d_x_first, d_norm_one = jax.vjp(rms_norm, x_flat, norm_one)[1](d_normed_one)
    d_input = (d_x_one + d_x_first).astype(jnp.bfloat16)
    d_qkv = [outer_sum(normed_one, d) for d in (d_query, d_key, d_value)]
    pieces = []
    for c in range(8):
        cols = slice(256 * c, 256 * c + 256)
        down = jnp.concatenate([d_down[cols, 256 * j : 256 * j + 256] for j in range(3)])
        pieces += [d_gate_w[:, cols], d_up_w[:, cols], down]
    pieces += [d_out_w[:, 256 * j : 256 * j + 256] for j in range(3)]
    for j in range(3):
        pieces += [d[:, 256 * j : 256 * j + 256] for d in d_qkv]
    stacked = jnp.stack([halves(p) for p in pieces]).reshape(NC, NT, 2, PIECE, 128)
    summed, y_back, dx_back = sum_all(stacked, result, d_input, row_bits, count)
    gains = lax.psum(jnp.stack([d_norm_one, d_norm_two]), ("seq", "rows"))
    summed = summed.astype(jnp.float32)
    parts = [[whole(summed[c, t]) for t in range(NT)] for c in range(NC)]
    g_gate = jnp.concatenate([parts[c][0] for c in range(8)], axis=1)
    g_up = jnp.concatenate([parts[c][1] for c in range(8)], axis=1)
    g_down = jnp.concatenate([parts[c][2].reshape(3, 256, 256).transpose(1, 0, 2).reshape(256, 768) for c in range(8)], axis=0)
    g_out = jnp.concatenate(parts[8], axis=1)
    g_q, g_k, g_v = (jnp.concatenate([parts[9 + j][t] for j in range(3)], axis=1) for t in range(NT))
    return (y_back, dx_back, g_q, g_k, g_v, g_out, gains[0], gains[1], g_gate, g_up, g_down)


def solution(mesh):
    split = P("rows", "seq", None)
    row_bits = (mesh.shape["rows"] - 1).bit_length()
    return jax.shard_map(
        partial(body, row_bits),
        mesh=mesh,
        in_specs=(split, P("rows", "seq"), split) + (P(),) * 9,
        out_specs=(split, split) + (P(),) * 9,
        check_vma=False,
    )
```

```python
from functools import partial

import jax
import jax.numpy as jnp
from jax import lax
from jax.experimental import pallas as pl
from jax.experimental.pallas import tpu as pltpu
from jax.sharding import PartitionSpec as P

MESH = pl.DeviceIdType.MESH
HEAD_DIM = 64
EPSILON = 1e-06
MASKED = -1000000000.0
PIECE = 768
NT = 3
COLS = 256
SLOTS = 3
BF = jnp.bfloat16
F32 = jnp.float32
NN = (((1,), (0,)), ((), ()))
NTRANS = (((1,), (1,)), ((), ()))


def dot(left, right, dims=NN):
    return lax.dot_general(left, right, dims, preferred_element_type=F32)


def flip(index, bit):
    unit = 1 << bit
    own = lax.rem(index // unit, 2)
    return own, index + (1 - 2 * own) * unit


class Links:
    def __init__(self, row_bits):
        seq, row = lax.axis_index("seq"), lax.axis_index("rows")
        self.seq, self.row = seq, row
        self.core, other = flip(seq, 0)
        self.other_core = (other, row)
        x_bit, x_other = flip(seq, 1)
        diagonal = flip(other, 1)[1]
        self.peers = [seq, other, x_other, diagonal]
        dims = [(x_bit, (x_other, row))]
        for bit in range(row_bits):
            own, partner = flip(row, bit)
            dims.append((own, (seq, partner)))
        self.halving = dims[:3]
        self.extra = dims[3:]
        n = len(self.halving)
        orders = [(0, 1, 2), (1, 2, 0), (2, 0, 1)]
        self.orders = [[d for d in order if d < n] for order in orders]

    def all(self):
        return [self.other_core] + [p for _, p in self.halving + self.extra]

    def greet(self):
        barrier = pltpu.get_barrier_semaphore()
        whom = self.all() + [(self.peers[3], self.row)]
        for partner in whom:
            pl.semaphore_signal(barrier, inc=1, device_id=partner, device_id_type=MESH)
        pl.semaphore_wait(barrier, len(whom))


class Reducer:
    def __init__(self, links, grads, landing, small, send, recv, free):
        self.l, self.g, self.landing, self.small = links, grads, landing, small
        self.send, self.recv, self.free = send, recv, free
        n, e = len(links.halving), len(links.extra)
        self.n, self.e = n, e
        self.steps = 2 + 2 * n + e + 1

    def span(self, t, level):
        low = 0
        for k in range(level):
            low = low + self.l.halving[self.l.orders[t][k]][0] * (PIECE >> (k + 1))
        return low if level == 0 else pl.multiple_of(low, 16)

    def copies(self, c, stage):
        l, n, e = self.l, self.n, self.e
        core, slot = l.core, lax.rem(c, SLOTS)
        if stage == 0:
            dst = self.landing.at[slot, :, pl.ds(0, PIECE)]
            return [self.make(self.g.at[c, :, 1 - core], dst, c, stage, 0, l.other_core)]
        if stage <= n:
            out = []
            for t in range(NT):
                own, partner = l.halving[l.orders[t][stage - 1]]
                rows = PIECE >> stage
                low = pl.multiple_of(self.span(t, stage - 1) + (1 - own) * rows, 16)
                src = self.g.at[c, t, core, pl.ds(low, rows)]
                dst = self.landing.at[slot, t, pl.ds(2 * PIECE - 2 * rows, rows)]
                out.append(self.make(src, dst, c, stage, t, partner))
            return out
        rows = PIECE >> n
        if stage <= n + e:
            partner = l.extra[stage - n - 1][1]
            out = []
            for t in range(NT):
                src = self.g.at[c, t, core, pl.ds(self.span(t, n), rows)]
                out.append(self.make(src, self.small.at[slot, stage - n - 1, t], c, stage, t, partner))
            return out
        k = 2 * n + e + 1 - stage
        if k > 0:
            out = []
            for t in range(NT):
                view = self.g.at[c, t, core, pl.ds(self.span(t, k), PIECE >> k)]
                out.append(self.make(view, view, c, stage, t, l.halving[l.orders[t][k - 1]][1]))
            return out
        view = self.g.at[c, :, core]
        return [self.make(view, view, c, stage, 0, l.other_core)]

    def make(self, src, dst, c, stage, t, partner):
        slot = lax.rem(c, SLOTS)
        return pltpu.make_async_remote_copy(
            src_ref=src, dst_ref=dst, send_sem=self.send.at[slot, stage, t], recv_sem=self.recv.at[slot, stage, t],
            device_id=partner, device_id_type=MESH)

    def fold(self, c, stage):
        n, e = self.n, self.e
        if stage > n + e:
            return
        core, slot = self.l.core, lax.rem(c, SLOTS)
        rows = PIECE >> min(stage, n)
        for t in range(NT):
            view = self.g.at[c, t, core, pl.ds(self.span(t, min(stage, n)), rows)]
            if stage <= n:
                got = self.landing[slot, t, pl.ds(0 if stage == 0 else 2 * PIECE - 2 * rows, rows)]
            else:
                got = self.small[slot, stage - n - 1, t]
            view[...] = (view[...].astype(F32) + got.astype(F32)).astype(BF)

    def partners(self, level):
        if level == 0:
            return [(0, self.l.other_core)]
        return [(t, self.l.halving[self.l.orders[t][level - 1]][1]) for t in range(NT)]

    def step(self, k, c):
        if k > 0:
            for copy in self.copies(c, k - 1):
                copy.wait()
            self.fold(c, k - 1)
            if k - 1 <= self.n:
                for t, partner in self.partners(k - 1):
                    pl.semaphore_signal(self.free.at[k - 1, t], inc=1, device_id=partner, device_id_type=MESH)
        if k < self.steps - 1:
            back = 2 * self.n + self.e + 1 - k
            if back <= self.n:
                for t, _ in self.partners(back):
                    pl.semaphore_wait(self.free.at[back, t], 1)
            for copy in self.copies(c, k):
                copy.start()

    def round(self, r, plan, finish):
        for k in reversed(range(self.steps)):
            c, valid = plan(r - k)

            @pl.when(valid)
            def _():
                self.step(k, c)
                if k == self.steps - 1:
                    finish(c)


def reducer_scratch(row_bits, chunks):
    n, e = min(3, row_bits + 1), max(0, row_bits - 2)
    stages = 2 + 2 * n + e
    return [
        pltpu.VMEM((chunks, NT, 2, PIECE, 128), BF),
        pltpu.VMEM((SLOTS, NT, 2 * PIECE - (PIECE >> n), 128), BF),
        pltpu.VMEM((SLOTS, max(e, 1), NT, PIECE >> n, 128), BF),
        pltpu.SemaphoreType.DMA((SLOTS, stages, NT)),
        pltpu.SemaphoreType.DMA((SLOTS, stages, NT)),
        pltpu.SemaphoreType.REGULAR((n + 1, NT)),
    ]


def half_of(pair, which):
    lane = lax.broadcasted_iota(jnp.int32, pair.shape, 1)
    return jnp.where((lane // HEAD_DIM) == which, pair, jnp.zeros_like(pair))


def inverse_rms(value):
    return lax.rsqrt(jnp.mean(value * value, axis=-1, keepdims=True) + EPSILON)


def layer_kernel(
    row_bits, sizes,
    blocks, ids, cotangent, w_qkv_hbm, w_out_hbm, gain_one, gain_two, w_gate, w_up, w_down,
    y_back, dx_back, summed, gain_sums,
    x_in, g_in, id_rows, id_q, id_k, n1_t, q, k, v, o_t, lse, x_one, n2, n2_t, acc, d_one, sent, part, w_qkv, w_out, gate_buf, up_buf, down_buf,
    dk_acc, dv_acc, gains, gains_in,
    grads, landing, small, send, recv, free,
    w_sem, ff_sem, own_sem, row_send, row_recv, out_sem, gain_send, gain_recv,
):
    tokens, positions, features, hidden, heads = sizes
    ff_chunks, groups, pairs = hidden // COLS, features // COLS, heads // 2
    count = tokens // positions
    out_chunk = ff_chunks
    chunks = ff_chunks + 1 + groups
    scale = HEAD_DIM ** (-0.5)
    scale_two = scale * 1.4426950408889634
    links = Links(row_bits)
    seq, row = links.seq, links.row
    reducer = Reducer(links, grads, landing, small, send, recv, free)

    def tile_of(d):
        return pl.ds(pl.multiple_of(links.peers[d] * positions, positions), positions)

    loads = [pltpu.make_async_copy(w_qkv_hbm.at[i], w_qkv.at[i], w_sem.at[i]) for i in range(3)]
    loads.append(pltpu.make_async_copy(w_out_hbm, w_out, w_sem.at[3]))
    mine = tile_of(0)
    own_ids = pl.ds(pl.multiple_of(seq * 8, 8), 8)
    own = [
        pltpu.make_async_copy(blocks.at[seq], x_in.at[mine], own_sem.at[0]),
        pltpu.make_async_copy(ids.at[seq], id_rows.at[own_ids], own_sem.at[1]),
        pltpu.make_async_copy(cotangent.at[seq], g_in.at[mine], own_sem.at[2]),
    ]
    own[0].start()
    for copy in loads:
        copy.start()
    own[1].start()
    own[2].start()
    links.greet()

    def to_peer(a, d, src, dst):
        return pltpu.make_async_remote_copy(
            src_ref=src, dst_ref=dst, send_sem=row_send.at[a, d], recv_sem=row_recv.at[a, d],
            device_id=(links.peers[d], row), device_id_type=MESH)

    x_moves = [to_peer(0, d, blocks.at[links.peers[d]], x_in.at[mine]) for d in range(1, count)]
    id_moves = [to_peer(1, d, ids.at[links.peers[d]], id_rows.at[own_ids]) for d in range(1, count)]
    g_moves = [to_peer(2, d, cotangent.at[links.peers[d]], g_in.at[mine]) for d in range(1, count)]
    for copy in x_moves + id_moves:
        copy.start()

    own[0].wait()
    for copy in loads[:3]:
        copy.wait()
    for d in range(count):
        if d > 0:
            x_moves[d - 1].wait()
        if d == count - 1:
            for copy in g_moves:
                copy.start()
        tile = tile_of(d)
        value = x_in[tile, :].astype(F32)
        normed = (value * inverse_rms(value) * gain_one[...]).astype(BF)
        n1_t[:, tile] = normed.T
        for i, made in enumerate((q, k, v)):
            made[tile, :] = dot(normed, w_qkv[i]).astype(BF)

    own[1].wait()
    for copy in id_moves:
        copy.wait()
    for d in range(count):
        id_q[:, positions * d : positions * (d + 1)] = id_rows[8 * d : 8 * d + 8, :]
    for j in range(tokens // 128):
        block = jnp.broadcast_to(id_q[0:1, 128 * j : 128 * j + 128], (128, 128))
        id_k[128 * j : 128 * j + 128, :] = block.T

    def masked(scores, queries, width):
        same = jnp.concatenate([id_k[...]] * (width // 128), axis=1) == id_q[0:1, queries]
        return jnp.where(same, scores, MASKED)

    def forward_pair(p, _):
        cols = pl.ds(pl.multiple_of(p * 128, 128), 128)
        key_pair = k[:, cols]
        value_t = v[:, cols].T
        for h in range(2):
            key = half_of(key_pair, h)
            rows = pl.ds(pl.multiple_of(p * 128 + HEAD_DIM * h, HEAD_DIM), HEAD_DIM)
            scores = masked(dot(key, q[:, cols], NTRANS) * scale_two, slice(None), tokens)
            largest = jnp.max(scores, axis=0, keepdims=True)
            exponent = jnp.exp2(scores - largest)
            total = jnp.sum(exponent, axis=0, keepdims=True)
            mixed = dot(value_t[HEAD_DIM * h : HEAD_DIM * (h + 1)], exponent.astype(BF))
            o_t[rows, :] = (mixed / total).astype(BF)
            lse[p * 2 + h, 0:1, :] = largest + jnp.log2(total)
        return 0

    lax.fori_loop(0, pairs, forward_pair, 0)

    def ff_loads(c):
        slot = lax.rem(c, 2)
        cols = pl.ds(pl.multiple_of(c * COLS, COLS), COLS)
        return [
            pltpu.make_async_copy(w_gate.at[:, cols], gate_buf.at[slot], ff_sem.at[slot, 0]),
            pltpu.make_async_copy(w_up.at[:, cols], up_buf.at[slot], ff_sem.at[slot, 1]),
            pltpu.make_async_copy(w_down.at[cols, :], down_buf.at[slot], ff_sem.at[slot, 2]),
        ]

    for copy in ff_loads(0):
        copy.start()

    loads[3].wait()

    def project_tile(i, _):
        tile = pl.ds(pl.multiple_of(i * positions, positions), positions)
        mixed = o_t[:, tile].T
        value = x_in[tile, :].astype(F32) + dot(mixed, w_out[...])
        normed = (value * inverse_rms(value) * gain_two[...]).astype(BF)
        x_one[tile, :] = value
        acc[tile, :] = value
        n2[tile, :] = normed
        n2_t[:, tile] = normed.T
        d_one[tile, :] = jnp.zeros((positions, features), F32)
        return 0

    lax.fori_loop(0, count, project_tile, 0)
    own[2].wait()
    for copy in g_moves:
        copy.wait()

    first = out_chunk + 2

    def plan(u):
        late = u - first
        chunk = jnp.where(u <= out_chunk, u, out_chunk + 1 + late // 2)
        valid = (u >= 0) & ((u <= out_chunk) | ((late >= 0) & (late <= 2 * (groups - 1)) & (lax.rem(late, 2) == 0)))
        return chunk, valid

    def finish(c):
        pltpu.make_async_copy(grads.at[c], summed.at[c], out_sem.at[c]).start()

    def put(c, t, piece):
        for half in range(2):
            grads[c, t, half] = piece[:, 128 * half : 128 * half + 128].astype(BF)

    half_tokens = tokens // 2

    def ff_chunk(c, _):
        slot = lax.rem(c, 2)

        @pl.when(c + 1 < ff_chunks)
        def _():
            for copy in ff_loads(c + 1):
                copy.start()

        for copy in ff_loads(c):
            copy.wait()
        for i in range(2):
            tile = slice(half_tokens * i, half_tokens * (i + 1))
            gate = dot(n2[tile, :], gate_buf[slot])
            up = dot(n2[tile, :], up_buf[slot])
            d_hidden = dot(g_in[tile, :], down_buf[slot], NTRANS)
            square = gate * gate
            bend = 0.7978845608028654 * 0.044715
            turn = jnp.tanh(gate * (0.7978845608028654 + bend * square))
            rise = 0.5 + 0.5 * turn
            activated = gate * rise
            slope = rise + 0.5 * gate * (1.0 - turn * turn) * (0.7978845608028654 + 3.0 * bend * square)
            low_h = (activated * up).astype(BF)
            low_gate = (d_hidden * up * slope).astype(BF)
            low_up = (d_hidden * activated).astype(BF)
            part[0, tile, :] = low_gate
            part[1, tile, :] = low_up
            part[2, tile, :] = low_h
            acc[tile, :] += dot(low_h, down_buf[slot])
            d_one[tile, :] += dot(low_gate, gate_buf[slot], NTRANS) + dot(low_up, up_buf[slot], NTRANS)
        put(c, 0, dot(n2_t[...], part[0]))
        put(c, 1, dot(n2_t[...], part[1]))
        made = dot(part[2].T, g_in[...])
        for j in range(NT):
            for half in range(2):
                at = COLS * j + 128 * half
                grads[c, 2, half, COLS * j : COLS * (j + 1), :] = made[:, at : at + 128].astype(BF)
        reducer.round(c, plan, finish)
        return 0

    lax.fori_loop(0, ff_chunks, ff_chunk, 0)

    gains[...] = jnp.zeros_like(gains)
    local = []
    y_moves = []
    for d in range(count):
        tile = tile_of(d)
        sent[tile, :] = acc[tile, :].astype(BF)
        if d == 0:
            copy = pltpu.make_async_copy(sent.at[tile], y_back.at[seq], own_sem.at[0])
            local.append(copy)
        else:
            copy = to_peer(0, d, sent.at[tile], y_back.at[seq])
            y_moves.append(copy)
        copy.start()
    for d in range(count):
        tile = tile_of(d)
        value = x_one[tile, :]
        inverse = inverse_rms(value)
        slope = d_one[tile, :]
        hat = value * inverse
        gains[1:2, :] += jnp.sum(slope * hat, axis=0, keepdims=True)
        weighted = slope * gain_two[...]
        pulled = inverse * (weighted - hat * jnp.mean(weighted * hat, axis=-1, keepdims=True))
        total = g_in[tile, :].astype(F32) + pulled
        d_one[tile, :] = total
        low = total.astype(BF)
        g_in[tile, :] = low
        d_mixed = dot(low, w_out[...], NTRANS).astype(BF)
        n2[tile, :] = d_mixed
        n2_t[:, tile] = d_mixed.T
    for t in range(NT):
        put(out_chunk, t, dot(o_t[...], g_in[:, COLS * t : COLS * (t + 1)]))
    reducer.round(jnp.int32(out_chunk), plan, finish)

    width = 256

    def backward_pair(step, _):
        g, j = step // 2, lax.rem(step, 2)
        cols = pl.ds(pl.multiple_of(step * 128, 128), 128)
        key_pair, value_pair = k[:, cols], v[:, cols]
        key_t = key_pair.T
        dq = []
        for h in range(2):
            key, value = half_of(key_pair, h), half_of(value_pair, h)
            rows = pl.ds(pl.multiple_of(step * 128 + HEAD_DIM * h, HEAD_DIM), HEAD_DIM)
            dq_parts = []
            for i in range(tokens // width):
                qs = slice(width * i, width * (i + 1))
                scores = masked(dot(key, q[qs, cols], NTRANS) * scale_two, qs, width)
                prob = jnp.exp2(scores - lse[step * 2 + h, 0:1, qs])
                delta = jnp.sum(n2_t[rows, qs].astype(F32) * o_t[rows, qs].astype(F32), axis=0, keepdims=True)
                d_prob = dot(value, n2[qs, cols], NTRANS)
                d_score = (prob * (d_prob - delta)).astype(BF)
                low = prob.astype(BF)
                dv = dot(low, n2[qs, cols])
                dk = dot(d_score, q[qs, cols])
                if i == 0:
                    dv_acc[h] = dv
                    dk_acc[h] = dk
                else:
                    dv_acc[h] += dv
                    dk_acc[h] += dk
                dq_parts.append((dot(key_t[HEAD_DIM * h : HEAD_DIM * (h + 1)], d_score) * scale).astype(BF))
            dq.append(jnp.concatenate(dq_parts, axis=1))
        lane = lax.broadcasted_iota(jnp.int32, (tokens, 128), 1) < HEAD_DIM
        at = pl.ds(pl.multiple_of(j * 128, 128), 128)
        part[0, :, at] = jnp.concatenate(dq, axis=0).T
        part[1, :, at] = (jnp.where(lane, dk_acc[0], dk_acc[1]) * scale).astype(BF)
        part[2, :, at] = jnp.where(lane, dv_acc[0], dv_acc[1]).astype(BF)

        @pl.when(j == 1)
        def _():
            group = pl.ds(pl.multiple_of(g * COLS, COLS), COLS)
            for t in range(NT):
                put(out_chunk + 1 + g, t, dot(n1_t[...], part[t]))
            for d in range(count):
                tile = slice(positions * d, positions * (d + 1))
                back = sum(dot(part[t, tile, :], w_qkv[t, :, group], NTRANS) for t in range(NT))

                @pl.when(g == 0)
                def _():
                    acc[tile, :] = back

                @pl.when(g > 0)
                def _():
                    acc[tile, :] += back

        reducer.round(out_chunk + 1 + step, plan, finish)
        return 0

    lax.fori_loop(0, pairs, backward_pair, 0)

    for copy in local + y_moves:
        copy.wait()
    dx_moves = []
    for d in range(count):
        tile = tile_of(d)
        value = x_in[tile, :].astype(F32)
        inverse = inverse_rms(value)
        slope = acc[tile, :]
        hat = value * inverse
        gains[0:1, :] += jnp.sum(slope * hat, axis=0, keepdims=True)
        weighted = slope * gain_one[...]
        pulled = inverse * (weighted - hat * jnp.mean(weighted * hat, axis=-1, keepdims=True))
        sent[tile, :] = (d_one[tile, :] + pulled).astype(BF)
        if d == 0:
            copy = pltpu.make_async_copy(sent.at[tile], dx_back.at[seq], own_sem.at[1])
        else:
            copy = to_peer(1, d, sent.at[tile], dx_back.at[seq])
        copy.start()
        dx_moves.append(copy)

    axes = links.all()

    def gain_copy(i):
        return pltpu.make_async_remote_copy(
            src_ref=gains, dst_ref=gains_in.at[i], send_sem=gain_send.at[i], recv_sem=gain_recv.at[i],
            device_id=axes[i], device_id_type=MESH)

    begin = out_chunk + 1 + pairs
    last = first + 2 * (groups - 1) + reducer.steps - 1

    def tail(r, _):
        for i in range(len(axes) + 1):

            @pl.when(r == begin + i)
            def _():
                if i > 0:
                    gain_copy(i - 1).wait()
                    gains[...] += gains_in[i - 1]
                if i < len(axes):
                    gain_copy(i).start()

        reducer.round(r, plan, finish)
        return 0

    lax.fori_loop(begin, max(last + 1, begin + len(axes) + 1), tail, 0)
    gain_sums[...] = gains[...]
    for copy in dx_moves:
        copy.wait()
    for c in range(chunks):
        pltpu.make_async_copy(grads.at[c], summed.at[c], out_sem.at[c]).wait()


def run_layer(row_bits, blocks, ids, cotangent, w_qkv, w_out, gain_one, gain_two, w_gate, w_up, w_down):
    count, positions, features = blocks.shape
    hidden = w_gate.shape[1]
    tokens, heads = count * positions, features // HEAD_DIM
    chunks = hidden // COLS + 1 + features // COLS
    axes = row_bits + 2
    sizes = (tokens, positions, features, hidden, heads)
    anywhere, inside = pl.BlockSpec(memory_space=pl.ANY), pl.BlockSpec(memory_space=pltpu.VMEM)
    back = jax.ShapeDtypeStruct(blocks.shape, BF)
    low = pltpu.VMEM((tokens, features), BF)
    turned = pltpu.VMEM((features, tokens), BF)
    full = pltpu.VMEM((tokens, features), F32)
    dma = pltpu.SemaphoreType.DMA
    return pl.pallas_call(
        partial(layer_kernel, row_bits, sizes),
        out_shape=(back, back, jax.ShapeDtypeStruct((chunks, NT, 2, PIECE, 128), BF), jax.ShapeDtypeStruct((8, features), F32)),
        in_specs=[anywhere] * 5 + [inside] * 2 + [anywhere] * 3,
        out_specs=[anywhere] * 3 + [inside],
        scratch_shapes=[
            low, low,
            pltpu.VMEM((count * 8, positions), jnp.int32), pltpu.VMEM((8, tokens), jnp.int32), pltpu.VMEM((tokens, 128), jnp.int32),
            turned, low, low, low, turned, pltpu.VMEM((heads, 8, tokens), F32), full, low, turned, full, full, low,
            pltpu.VMEM((NT, tokens, COLS), BF),
            pltpu.VMEM((3, features, features), BF), pltpu.VMEM((features, features), BF),
            pltpu.VMEM((2, features, COLS), BF), pltpu.VMEM((2, features, COLS), BF), pltpu.VMEM((2, COLS, features), BF),
            pltpu.VMEM((2, tokens, 128), F32), pltpu.VMEM((2, tokens, 128), F32),
            pltpu.VMEM((8, features), F32), pltpu.VMEM((axes, 8, features), F32),
        ] + reducer_scratch(row_bits, chunks) + [
            dma((4,)), dma((2, 3)), dma((3,)), dma((3, count)), dma((3, count)), dma((chunks,)), dma((axes,)), dma((axes,)),
        ],
        compiler_params=pltpu.CompilerParams(collective_id=0, has_side_effects=True, vmem_limit_bytes=63 * 2**20),
        cost_estimate=pl.CostEstimate(flops=60 * 10**9, bytes_accessed=60 * 10**6, transcendentals=10**7),
    )(blocks, ids, cotangent, w_qkv, w_out, gain_one, gain_two, w_gate, w_up, w_down)


def widen_ff_kernel(low, gate, up, down):
    for half in range(2):
        cols = slice(128 * half, 128 * half + 128)
        gate[:, cols] = low[0, 0, half].astype(F32)
        up[:, cols] = low[0, 1, half].astype(F32)
        for j in range(NT):
            down[:, COLS * j + 128 * half : COLS * j + 128 * half + 128] = low[0, 2, half, COLS * j : COLS * (j + 1), :].astype(F32)


def widen_ff(summed, features, hidden):
    return pl.pallas_call(
        widen_ff_kernel,
        grid=(hidden // COLS,),
        out_shape=(jax.ShapeDtypeStruct((features, hidden), F32),) * 2 + (jax.ShapeDtypeStruct((hidden, features), F32),),
        in_specs=[pl.BlockSpec((1, NT, 2, PIECE, 128), lambda c: (c, 0, 0, 0, 0))],
        out_specs=[pl.BlockSpec((features, COLS), lambda c: (0, c))] * 2 + [pl.BlockSpec((COLS, features), lambda c: (c, 0))],
    )(summed)


def widen_square_kernel(low_out, low_qkv, g_out, g_q, g_k, g_v):
    for half in range(2):
        cols = slice(128 * half, 128 * half + 128)
        g_out[:, cols] = low_out[0, 0, half].astype(F32)
        for t, made in enumerate((g_q, g_k, g_v)):
            made[:, cols] = low_qkv[0, t, half].astype(F32)


def widen_square(summed, features, first):
    wide = pl.BlockSpec((features, COLS), lambda j: (0, j))
    return pl.pallas_call(
        widen_square_kernel,
        grid=(features // COLS,),
        out_shape=(jax.ShapeDtypeStruct((features, features), F32),) * 4,
        in_specs=[
            pl.BlockSpec((1, 1, 2, PIECE, 128), lambda j: (first, j, 0, 0, 0)),
            pl.BlockSpec((1, NT, 2, PIECE, 128), lambda j: (first + 1 + j, 0, 0, 0, 0)),
        ],
        out_specs=[wide] * 4,
    )(summed, summed)


def body(row_bits, blocks, segment_ids, cotangent, w_query, w_key, w_value, w_out, norm_one, norm_two, w_gate, w_up, w_down):
    count, positions, features = blocks.shape
    hidden = w_gate.shape[1]
    ids = jnp.broadcast_to(segment_ids[:, None, :], (count, 8, positions))
    y, dx, summed, gains = run_layer(
        row_bits, blocks, ids, cotangent, jnp.stack([w_query, w_key, w_value]), w_out,
        norm_one.reshape(1, features), norm_two.reshape(1, features), w_gate, w_up, w_down)
    g_gate, g_up, g_down = widen_ff(summed, features, hidden)
    g_out, g_q, g_k, g_v = widen_square(summed, features, hidden // COLS)
    return (y, dx, g_q, g_k, g_v, g_out, gains[0], gains[1], g_gate, g_up, g_down)


def solution(mesh):
    split = P("rows", "seq", None)
    row_bits = (mesh.shape["rows"] - 1).bit_length()
    return jax.shard_map(
        partial(body, row_bits),
        mesh=mesh,
        in_specs=(split, P("rows", "seq"), split) + (P(),) * 9,
        out_specs=(split, split) + (P(),) * 9,
        check_vma=False,
    )
```

```python
from functools import partial

import jax
import jax.numpy as jnp
from jax import lax
from jax.experimental import pallas as pl
from jax.experimental.pallas import tpu as pltpu
from jax.sharding import PartitionSpec as P

MESH = pl.DeviceIdType.MESH
HEAD_DIM = 64
EPSILON = 1e-06
MASKED = -1000000000.0
PIECE = 768
NT = 3
COLS = 256
SLOTS = 4
GAP = 2
Y_PIECES = 8
X_PIECES = 16
BF = jnp.bfloat16
F32 = jnp.float32
NN = (((1,), (0,)), ((), ()))
NTRANS = (((1,), (1,)), ((), ()))


def dot(left, right, dims=NN):
    return lax.dot_general(left, right, dims, preferred_element_type=F32)


def flip(index, bit):
    unit = 1 << bit
    own = lax.rem(index // unit, 2)
    return own, index + (1 - 2 * own) * unit


class Links:
    def __init__(self, row_bits):
        seq, row = lax.axis_index("seq"), lax.axis_index("rows")
        self.seq, self.row = seq, row
        self.core, other = flip(seq, 0)
        self.other_core = (other, row)
        x_bit, x_other = flip(seq, 1)
        diagonal = flip(other, 1)[1]
        self.peers = [seq, other, x_other, diagonal]
        dims = [(x_bit, (x_other, row))]
        for bit in range(row_bits):
            own, partner = flip(row, bit)
            dims.append((own, (seq, partner)))
        self.halving = dims[:3]
        self.extra = dims[3:]
        n = len(self.halving)
        orders = [(0, 1, 2), (1, 2, 0), (2, 0, 1)]
        self.orders = [[d for d in order if d < n] for order in orders]

    def all(self):
        return [self.other_core] + [p for _, p in self.halving + self.extra]

    def greet(self):
        barrier = pltpu.get_barrier_semaphore()
        whom = self.all() + [(self.peers[3], self.row)]
        for partner in whom:
            pl.semaphore_signal(barrier, inc=1, device_id=partner, device_id_type=MESH)
        pl.semaphore_wait(barrier, len(whom))


class Reducer:
    def __init__(self, links, grads, landing, small, send, recv, free):
        self.l, self.g, self.landing, self.small = links, grads, landing, small
        self.send, self.recv, self.free = send, recv, free
        n, e = len(links.halving), len(links.extra)
        self.n, self.e = n, e

    def span(self, t, level):
        low = 0
        for k in range(level):
            low = low + self.l.halving[self.l.orders[t][k]][0] * (PIECE >> (k + 1))
        return low if level == 0 else pl.multiple_of(low, 16)

    def copies(self, c, stage):
        l, n, e = self.l, self.n, self.e
        core, slot = l.core, lax.rem(c, SLOTS)
        if stage == 0:
            dst = self.landing.at[slot, :, pl.ds(0, PIECE)]
            return [self.make(self.g.at[c, :, 1 - core], dst, c, stage, 0, l.other_core)]
        if stage <= n:
            out = []
            for t in range(NT):
                own, partner = l.halving[l.orders[t][stage - 1]]
                rows = PIECE >> stage
                low = pl.multiple_of(self.span(t, stage - 1) + (1 - own) * rows, 16)
                src = self.g.at[c, t, core, pl.ds(low, rows)]
                dst = self.landing.at[slot, t, pl.ds(2 * PIECE - 2 * rows, rows)]
                out.append(self.make(src, dst, c, stage, t, partner))
            return out
        rows = PIECE >> n
        if stage <= n + e:
            partner = l.extra[stage - n - 1][1]
            out = []
            for t in range(NT):
                src = self.g.at[c, t, core, pl.ds(self.span(t, n), rows)]
                out.append(self.make(src, self.small.at[slot, stage - n - 1, t], c, stage, t, partner))
            return out
        k = 2 * n + e + 1 - stage
        if k > 0:
            out = []
            for t in range(NT):
                view = self.g.at[c, t, core, pl.ds(self.span(t, k), PIECE >> k)]
                out.append(self.make(view, view, c, stage, t, l.halving[l.orders[t][k - 1]][1]))
            return out
        view = self.g.at[c, :, core]
        return [self.make(view, view, c, stage, 0, l.other_core)]

    def make(self, src, dst, c, stage, t, partner):
        slot = lax.rem(c, SLOTS)
        return pltpu.make_async_remote_copy(
            src_ref=src, dst_ref=dst, send_sem=self.send.at[slot, stage, t], recv_sem=self.recv.at[slot, stage, t],
            device_id=partner, device_id_type=MESH)

    def fold(self, c, stage):
        n, e = self.n, self.e
        if stage > n + e:
            return
        core, slot = self.l.core, lax.rem(c, SLOTS)
        rows = PIECE >> min(stage, n)
        for t in range(NT):
            view = self.g.at[c, t, core, pl.ds(self.span(t, min(stage, n)), rows)]
            if stage <= n:
                got = self.landing[slot, t, pl.ds(0 if stage == 0 else 2 * PIECE - 2 * rows, rows)]
            else:
                got = self.small[slot, stage - n - 1, t]
            view[...] = view[...] + got

    def partners(self, level):
        if level == 0:
            return [(0, self.l.other_core)]
        return [(t, self.l.halving[self.l.orders[t][level - 1]][1]) for t in range(NT)]

    def shrink(self, k, c):
        if k > 0:
            for copy in self.copies(c, k - 1):
                copy.wait()
            self.fold(c, k - 1)
            if k - 1 <= self.n:
                for t, partner in self.partners(k - 1):
                    pl.semaphore_signal(self.free.at[k - 1, t], inc=1, device_id=partner, device_id_type=MESH)
        if k <= self.n + self.e:
            for copy in self.copies(c, k):
                copy.start()

    def spread(self, j, c):
        stage = self.n + self.e + 1 + j
        if j > 0:
            for copy in self.copies(c, stage - 1):
                copy.wait()
        if j <= self.n:
            for t, _ in self.partners(self.n - j):
                pl.semaphore_wait(self.free.at[self.n - j, t], 1)
            for copy in self.copies(c, stage):
                copy.start()

    def shrink_round(self, u, plan):
        for k in reversed(range(self.n + self.e + 2)):
            c, valid = plan(u - GAP * k)
            pl.when(valid)(partial(self.shrink, k, c))

    def spread_round(self, u, plan, finish):
        for j in reversed(range(self.n + 2)):
            c, valid = plan(u - GAP * j)

            @pl.when(valid)
            def _():
                self.spread(j, c)
                if j == self.n + 1:
                    finish(c)


def reducer_scratch(row_bits, chunks):
    n, e = min(3, row_bits + 1), max(0, row_bits - 2)
    stages = 2 + 2 * n + e
    return [
        pltpu.VMEM((chunks, NT, 2, PIECE, 128), BF),
        pltpu.VMEM((SLOTS, NT, 2 * PIECE - (PIECE >> n), 128), BF),
        pltpu.VMEM((SLOTS, max(e, 1), NT, PIECE >> n, 128), BF),
        pltpu.SemaphoreType.DMA((SLOTS, stages, NT)),
        pltpu.SemaphoreType.DMA((SLOTS, stages, NT)),
        pltpu.SemaphoreType.REGULAR((n + 1, NT)),
    ]


def half_of(pair, which):
    lane = lax.broadcasted_iota(jnp.int32, pair.shape, 1)
    return jnp.where((lane // HEAD_DIM) == which, pair, jnp.zeros_like(pair))


def inverse_rms(value):
    return lax.rsqrt(jnp.mean(value * value, axis=-1, keepdims=True) + EPSILON)


def layer_kernel(
    row_bits, sizes,
    blocks, ids, cotangent, w_q_hbm, w_k_hbm, w_v_hbm, w_out_hbm, gain_one, gain_two, w_gate, w_up, w_down,
    y_back, dx_back, summed, gain_sums,
    x_in, g_in, id_rows, id_q, id_k, n1_t, q, k, v, o_t, lse, x_one, n2, n2_t, acc, d_one, sent, part, w_qkv, w_out, gate_buf, up_buf, down_buf,
    dk_acc, dv_acc, gains, gains_in,
    grads, landing, small, send, recv, free,
    w_sem, ff_sem, own_sem, row_send, row_recv, out_sem, gain_send, gain_recv,
):
    tokens, positions, features, hidden, heads = sizes
    ff_chunks, groups, pairs = hidden // COLS, features // COLS, heads // 2
    count = tokens // positions
    out_chunk = ff_chunks
    chunks = ff_chunks + 1 + groups
    scale = HEAD_DIM ** (-0.5)
    scale_two = scale * 1.4426950408889634
    links = Links(row_bits)
    seq, row = links.seq, links.row
    reducer = Reducer(links, grads, landing, small, send, recv, free)

    def tile_of(d):
        return pl.ds(pl.multiple_of(links.peers[d] * positions, positions), positions)

    loads = [pltpu.make_async_copy(w, w_qkv.at[i], w_sem.at[i]) for i, w in enumerate((w_q_hbm, w_k_hbm, w_v_hbm))]
    loads.append(pltpu.make_async_copy(w_out_hbm, w_out, w_sem.at[3]))
    mine = tile_of(0)
    own = [
        pltpu.make_async_copy(blocks.at[seq], x_in.at[mine], own_sem.at[0]),
        pltpu.make_async_copy(ids, id_rows.at[seq], own_sem.at[1]),
        pltpu.make_async_copy(cotangent.at[seq], g_in.at[mine], own_sem.at[2]),
    ]
    own[0].start()
    for copy in loads:
        copy.start()
    own[1].start()
    own[2].start()
    links.greet()

    def to_peer(a, d, src, dst):
        return pltpu.make_async_remote_copy(
            src_ref=src, dst_ref=dst, send_sem=row_send.at[a, d], recv_sem=row_recv.at[a, d],
            device_id=(links.peers[d], row), device_id_type=MESH)

    x_moves = [to_peer(0, d, blocks.at[links.peers[d]], x_in.at[mine]) for d in range(1, count)]
    id_moves = [to_peer(1, d, ids, id_rows.at[seq]) for d in range(1, count)]
    g_moves = [to_peer(2, d, cotangent.at[links.peers[d]], g_in.at[mine]) for d in range(1, count)]
    for copy in x_moves + id_moves:
        copy.start()

    own[0].wait()
    for copy in loads[:3]:
        copy.wait()
    for d in range(count):
        if d > 0:
            x_moves[d - 1].wait()
        if d == count - 1:
            for copy in g_moves:
                copy.start()
        tile = tile_of(d)
        value = x_in[tile, :].astype(F32)
        normed = (value * inverse_rms(value) * gain_one[...].reshape(1, features)).astype(BF)
        n1_t[:, tile] = normed.T
        for i, made in enumerate((q, k, v)):
            made[tile, :] = dot(normed, w_qkv[i]).astype(BF)

    own[1].wait()
    for copy in id_moves:
        copy.wait()
    for d in range(count):
        id_q[0:1, positions * d : positions * (d + 1)] = id_rows[d, pl.ds(seq, 1), :]
    for j in range(tokens // 128):
        block = jnp.broadcast_to(id_q[0:1, 128 * j : 128 * j + 128], (128, 128))
        id_k[128 * j : 128 * j + 128, :] = block.T

    def masked(scores, queries, width):
        same = jnp.concatenate([id_k[...]] * (width // 128), axis=1) == id_q[0:1, queries]
        return jnp.where(same, scores, MASKED)

    def forward_pair(p, _):
        cols = pl.ds(pl.multiple_of(p * 128, 128), 128)
        key_pair = k[:, cols]
        value_t = v[:, cols].T
        for h in range(2):
            key = half_of(key_pair, h)
            rows = pl.ds(pl.multiple_of(p * 128 + HEAD_DIM * h, HEAD_DIM), HEAD_DIM)
            scores = masked(dot(key, q[:, cols], NTRANS) * scale_two, slice(None), tokens)
            largest = jnp.max(scores, axis=0, keepdims=True)
            exponent = jnp.exp2(scores - largest)
            total = jnp.sum(exponent, axis=0, keepdims=True)
            mixed = dot(value_t[HEAD_DIM * h : HEAD_DIM * (h + 1)], exponent.astype(BF))
            o_t[rows, :] = (mixed / total).astype(BF)
            lse[p * 2 + h, 0:1, :] = largest + jnp.log2(total)
        return 0

    lax.fori_loop(0, pairs, forward_pair, 0)

    def ff_loads(c):
        slot = lax.rem(c, 2)
        cols = pl.ds(pl.multiple_of(c * COLS, COLS), COLS)
        return [
            pltpu.make_async_copy(w_gate.at[:, cols], gate_buf.at[slot], ff_sem.at[slot, 0]),
            pltpu.make_async_copy(w_up.at[:, cols], up_buf.at[slot], ff_sem.at[slot, 1]),
            pltpu.make_async_copy(w_down.at[cols, :], down_buf.at[slot], ff_sem.at[slot, 2]),
        ]

    for copy in ff_loads(0):
        copy.start()

    loads[3].wait()

    def project_tile(i, _):
        tile = pl.ds(pl.multiple_of(i * positions, positions), positions)
        mixed = o_t[:, tile].T
        value = x_in[tile, :].astype(F32) + dot(mixed, w_out[...])
        normed = (value * inverse_rms(value) * gain_two[...].reshape(1, features)).astype(BF)
        x_one[tile, :] = value
        acc[tile, :] = value
        n2[tile, :] = normed
        n2_t[:, tile] = normed.T
        d_one[tile, :] = jnp.zeros((positions, features), F32)
        return 0

    lax.fori_loop(0, count, project_tile, 0)
    own[2].wait()
    for copy in g_moves:
        copy.wait()

    down = reducer.n + reducer.e + 1
    late_down = out_chunk + 4

    def shrink_plan(u):
        late = u - late_down
        chunk = jnp.where(u <= out_chunk, u, out_chunk + 1 + late // 4)
        valid = (u >= 0) & ((u <= out_chunk) | ((late >= 0) & (late <= 4 * (groups - 1)) & (lax.rem(late, 4) == 0)))
        return chunk, valid

    def spread_plan(u):
        return shrink_plan(u - GAP * down)

    def advance(u):
        reducer.shrink_round(u, shrink_plan)
        reducer.spread_round(u, spread_plan, finish)

    def finish(c):
        pltpu.make_async_copy(grads.at[c], summed.at[c], out_sem.at[c]).start()

    def put(c, t, piece):
        for half in range(2):
            grads[c, t, half] = piece[:, 128 * half : 128 * half + 128].astype(BF)

    half_tokens = tokens // 2

    def ff_chunk(c, _):
        slot = lax.rem(c, 2)

        @pl.when(c + 1 < ff_chunks)
        def _():
            for copy in ff_loads(c + 1):
                copy.start()

        for copy in ff_loads(c):
            copy.wait()
        for i in range(2):
            tile = slice(half_tokens * i, half_tokens * (i + 1))
            gate = dot(n2[tile, :], gate_buf[slot])
            up = dot(n2[tile, :], up_buf[slot])
            d_hidden = dot(g_in[tile, :], down_buf[slot], NTRANS)
            square = gate * gate
            bend = 0.7978845608028654 * 0.044715
            turn = jnp.tanh(gate * (0.7978845608028654 + bend * square))
            rise = 0.5 + 0.5 * turn
            activated = gate * rise
            slope = rise + 0.5 * gate * (1.0 - turn * turn) * (0.7978845608028654 + 3.0 * bend * square)
            low_h = (activated * up).astype(BF)
            low_gate = (d_hidden * up * slope).astype(BF)
            low_up = (d_hidden * activated).astype(BF)
            part[0, tile, :] = low_gate
            part[1, tile, :] = low_up
            part[2, tile, :] = low_h
            acc[tile, :] += dot(low_h, down_buf[slot])
            d_one[tile, :] += dot(low_gate, gate_buf[slot], NTRANS) + dot(low_up, up_buf[slot], NTRANS)
        put(c, 0, dot(n2_t[...], part[0]))
        put(c, 1, dot(n2_t[...], part[1]))
        made = dot(part[2].T, g_in[...])
        for j in range(NT):
            for half in range(2):
                at = COLS * j + 128 * half
                grads[c, 2, half, COLS * j : COLS * (j + 1), :] = made[:, at : at + 128].astype(BF)
        reducer.shrink_round(c, shrink_plan)
        return 0

    lax.fori_loop(0, ff_chunks, ff_chunk, 0)

    gains[...] = jnp.zeros_like(gains)
    for d in range(count):
        tile = tile_of(d)
        sent[tile, :] = acc[tile, :].astype(BF)

    def whole_back(a, dst):
        own_copy = pltpu.make_async_copy(sent.at[mine], dst.at[seq], own_sem.at[a])
        return [own_copy] + [to_peer(a, d, sent.at[tile_of(d)], dst.at[seq]) for d in range(1, count)]

    def piece_back(a, dst, i, pieces):
        rows = positions // pieces
        for d in range(2, count):
            low = pl.multiple_of(links.peers[d] * positions + i * rows, 16)
            to = pl.ds(pl.multiple_of(i * rows, 16), rows)
            to_peer(a, d, sent.at[pl.ds(low, rows)], dst.at[seq, to]).start()

    y_moves = whole_back(0, y_back)
    for copy in y_moves[:2]:
        copy.start()
    for d in range(count):
        tile = tile_of(d)
        value = x_one[tile, :]
        inverse = inverse_rms(value)
        slope = d_one[tile, :]
        hat = value * inverse
        gains[1:2, :] += jnp.sum(slope * hat, axis=0, keepdims=True)
        weighted = slope * gain_two[...].reshape(1, features)
        pulled = inverse * (weighted - hat * jnp.mean(weighted * hat, axis=-1, keepdims=True))
        total = g_in[tile, :].astype(F32) + pulled
        d_one[tile, :] = total
        low = total.astype(BF)
        g_in[tile, :] = low
        d_mixed = dot(low, w_out[...], NTRANS).astype(BF)
        n2[tile, :] = d_mixed
        n2_t[:, tile] = d_mixed.T
    for t in range(NT):
        put(out_chunk, t, dot(o_t[...], g_in[:, COLS * t : COLS * (t + 1)]))
    reducer.shrink_round(jnp.int32(out_chunk), shrink_plan)

    width = 256

    def backward_pair(step, _):
        g, j = step // 2, lax.rem(step, 2)
        cols = pl.ds(pl.multiple_of(step * 128, 128), 128)
        key_pair, value_pair = k[:, cols], v[:, cols]
        key_t = key_pair.T
        dq = []
        for h in range(2):
            key, value = half_of(key_pair, h), half_of(value_pair, h)
            rows = pl.ds(pl.multiple_of(step * 128 + HEAD_DIM * h, HEAD_DIM), HEAD_DIM)
            dq_parts = []
            for i in range(tokens // width):
                qs = slice(width * i, width * (i + 1))
                scores = masked(dot(key, q[qs, cols], NTRANS) * scale_two, qs, width)
                prob = jnp.exp2(scores - lse[step * 2 + h, 0:1, qs])
                delta = jnp.sum(n2_t[rows, qs].astype(F32) * o_t[rows, qs].astype(F32), axis=0, keepdims=True)
                d_prob = dot(value, n2[qs, cols], NTRANS)
                d_score = (prob * (d_prob - delta)).astype(BF)
                low = prob.astype(BF)
                dv = dot(low, n2[qs, cols])
                dk = dot(d_score, q[qs, cols])
                if i == 0:
                    dv_acc[h] = dv
                    dk_acc[h] = dk
                else:
                    dv_acc[h] += dv
                    dk_acc[h] += dk
                dq_parts.append((dot(key_t[HEAD_DIM * h : HEAD_DIM * (h + 1)], d_score) * scale).astype(BF))
            dq.append(jnp.concatenate(dq_parts, axis=1))
            if h == 0:
                advance(out_chunk + 1 + 2 * step)

                @pl.when(step < Y_PIECES // 2)
                def _():
                    piece_back(0, y_back, 2 * step, Y_PIECES)
        lane = lax.broadcasted_iota(jnp.int32, (tokens, 128), 1) < HEAD_DIM
        q[:, cols] = jnp.concatenate(dq, axis=0).T
        k[:, cols] = (jnp.where(lane, dk_acc[0], dk_acc[1]) * scale).astype(BF)
        v[:, cols] = jnp.where(lane, dv_acc[0], dv_acc[1]).astype(BF)

        @pl.when(j == 1)
        def _():
            group = pl.ds(pl.multiple_of(g * COLS, COLS), COLS)
            for t, made in enumerate((q, k, v)):
                put(out_chunk + 1 + g, t, dot(n1_t[...], made[:, group]))

        advance(out_chunk + 2 + 2 * step)

        @pl.when(step < Y_PIECES // 2)
        def _():
            piece_back(0, y_back, 2 * step + 1, Y_PIECES)

        return 0

    lax.fori_loop(0, pairs, backward_pair, 0)

    for copy in y_moves:
        copy.wait()
    dx_moves = whole_back(1, dx_back)
    for d in reversed(range(count)):
        tile = tile_of(d)
        slope = sum(dot(made[tile, :], w_qkv[t], NTRANS) for t, made in enumerate((q, k, v)))
        value = x_in[tile, :].astype(F32)
        inverse = inverse_rms(value)
        hat = value * inverse
        gains[0:1, :] += jnp.sum(slope * hat, axis=0, keepdims=True)
        weighted = slope * gain_one[...].reshape(1, features)
        pulled = inverse * (weighted - hat * jnp.mean(weighted * hat, axis=-1, keepdims=True))
        sent[tile, :] = (d_one[tile, :] + pulled).astype(BF)
    for copy in dx_moves[:2]:
        copy.start()

    axes = links.all()

    def gain_copy(i):
        return pltpu.make_async_remote_copy(
            src_ref=gains, dst_ref=gains_in.at[i], send_sem=gain_send.at[i], recv_sem=gain_recv.at[i],
            device_id=axes[i], device_id_type=MESH)

    begin = out_chunk + 1 + 2 * pairs
    last = late_down + 4 * (groups - 1) + GAP * (down + reducer.n + 1)

    def tail(r, _):
        for i in range(len(axes) + 1):

            @pl.when(r == begin + i)
            def _():
                if i > 0:
                    gain_copy(i - 1).wait()
                    gains[...] += gains_in[i - 1]
                if i < len(axes):
                    gain_copy(i).start()

        advance(r)

        @pl.when(r < begin + X_PIECES)
        def _():
            piece_back(1, dx_back, r - begin, X_PIECES)

        return 0

    lax.fori_loop(begin, max(last + 1, begin + max(len(axes) + 1, X_PIECES)), tail, 0)
    gain_sums[...] = gains[...]
    for copy in dx_moves:
        copy.wait()
    for c in range(chunks):
        pltpu.make_async_copy(grads.at[c], summed.at[c], out_sem.at[c]).wait()


def run_layer(row_bits, blocks, ids, cotangent, w_query, w_key, w_value, w_out, gain_one, gain_two, w_gate, w_up, w_down):
    count, positions, features = blocks.shape
    hidden = w_gate.shape[1]
    tokens, heads = count * positions, features // HEAD_DIM
    chunks = hidden // COLS + 1 + features // COLS
    axes = row_bits + 2
    sizes = (tokens, positions, features, hidden, heads)
    anywhere, inside = pl.BlockSpec(memory_space=pl.ANY), pl.BlockSpec(memory_space=pltpu.VMEM)
    back = jax.ShapeDtypeStruct(blocks.shape, BF)
    low = pltpu.VMEM((tokens, features), BF)
    turned = pltpu.VMEM((features, tokens), BF)
    full = pltpu.VMEM((tokens, features), F32)
    dma = pltpu.SemaphoreType.DMA
    return pl.pallas_call(
        partial(layer_kernel, row_bits, sizes),
        out_shape=(back, back, jax.ShapeDtypeStruct((chunks, NT, 2, PIECE, 128), BF), jax.ShapeDtypeStruct((8, features), F32)),
        in_specs=[anywhere] * 7 + [inside] * 2 + [anywhere] * 3,
        out_specs=[anywhere] * 3 + [inside],
        scratch_shapes=[
            low, low,
            pltpu.VMEM((count, count, positions), jnp.int32), pltpu.VMEM((8, tokens), jnp.int32), pltpu.VMEM((tokens, 128), jnp.int32),
            turned, low, low, low, turned, pltpu.VMEM((heads, 8, tokens), F32), full, low, turned, full, full, low,
            pltpu.VMEM((NT, tokens, COLS), BF),
            pltpu.VMEM((3, features, features), BF), pltpu.VMEM((features, features), BF),
            pltpu.VMEM((2, features, COLS), BF), pltpu.VMEM((2, features, COLS), BF), pltpu.VMEM((2, COLS, features), BF),
            pltpu.VMEM((2, tokens, 128), F32), pltpu.VMEM((2, tokens, 128), F32),
            pltpu.VMEM((8, features), F32), pltpu.VMEM((axes, 8, features), F32),
        ] + reducer_scratch(row_bits, chunks) + [
            dma((4,)), dma((2, 3)), dma((3,)), dma((3, count)), dma((3, count)), dma((chunks,)), dma((axes,)), dma((axes,)),
        ],
        compiler_params=pltpu.CompilerParams(collective_id=0, has_side_effects=True, vmem_limit_bytes=63 * 2**20),
        cost_estimate=pl.CostEstimate(flops=60 * 10**9, bytes_accessed=60 * 10**6, transcendentals=10**7),
    )(blocks, ids, cotangent, w_query, w_key, w_value, w_out, gain_one, gain_two, w_gate, w_up, w_down)


def widen_ff_kernel(low, gate, up, down):
    for half in range(2):
        cols = slice(128 * half, 128 * half + 128)
        gate[:, cols] = low[0, 0, half].astype(F32)
        up[:, cols] = low[0, 1, half].astype(F32)
        for j in range(NT):
            down[:, COLS * j + 128 * half : COLS * j + 128 * half + 128] = low[0, 2, half, COLS * j : COLS * (j + 1), :].astype(F32)


def widen_ff(summed, features, hidden):
    return pl.pallas_call(
        widen_ff_kernel,
        grid=(hidden // COLS,),
        out_shape=(jax.ShapeDtypeStruct((features, hidden), F32),) * 2 + (jax.ShapeDtypeStruct((hidden, features), F32),),
        in_specs=[pl.BlockSpec((1, NT, 2, PIECE, 128), lambda c: (c, 0, 0, 0, 0))],
        out_specs=[pl.BlockSpec((features, COLS), lambda c: (0, c))] * 2 + [pl.BlockSpec((COLS, features), lambda c: (c, 0))],
    )(summed)


def widen_square_kernel(low_out, low_qkv, g_out, g_q, g_k, g_v):
    for half in range(2):
        cols = slice(128 * half, 128 * half + 128)
        g_out[:, cols] = low_out[0, 0, half].astype(F32)
        for t, made in enumerate((g_q, g_k, g_v)):
            made[:, cols] = low_qkv[0, t, half].astype(F32)


def widen_square(summed, features, first):
    wide = pl.BlockSpec((features, COLS), lambda j: (0, j))
    return pl.pallas_call(
        widen_square_kernel,
        grid=(features // COLS,),
        out_shape=(jax.ShapeDtypeStruct((features, features), F32),) * 4,
        in_specs=[
            pl.BlockSpec((1, 1, 2, PIECE, 128), lambda j: (first, j, 0, 0, 0)),
            pl.BlockSpec((1, NT, 2, PIECE, 128), lambda j: (first + 1 + j, 0, 0, 0, 0)),
        ],
        out_specs=[wide] * 4,
    )(summed, summed)


def body(row_bits, blocks, segment_ids, cotangent, w_query, w_key, w_value, w_out, norm_one, norm_two, w_gate, w_up, w_down):
    features, hidden = w_gate.shape
    y, dx, summed, gains = run_layer(
        row_bits, blocks, segment_ids, cotangent, w_query, w_key, w_value, w_out, norm_one, norm_two, w_gate, w_up, w_down)
    g_gate, g_up, g_down = widen_ff(summed, features, hidden)
    g_out, g_q, g_k, g_v = widen_square(summed, features, hidden // COLS)
    return (y, dx, g_q, g_k, g_v, g_out, gains[0], gains[1], g_gate, g_up, g_down)


def solution(mesh):
    split = P("rows", "seq", None)
    row_bits = (mesh.shape["rows"] - 1).bit_length()
    return jax.shard_map(
        partial(body, row_bits),
        mesh=mesh,
        in_specs=(split, P("rows", "seq"), split) + (P(),) * 9,
        out_specs=(split, split) + (P(),) * 9,
        check_vma=False,
    )
```

```python
from functools import partial

import jax
import jax.numpy as jnp
from jax import lax
from jax.experimental import pallas as pl
from jax.experimental.pallas import tpu as pltpu
from jax.sharding import PartitionSpec as P

MESH = pl.DeviceIdType.MESH
HEAD_DIM = 64
EPSILON = 1e-06
MASKED = -1000000000.0
PIECE = 768
NT = 3
COLS = 256
SLOTS = 4
GAP = 2
Y_PIECES = 8
X_PIECES = 16
BF = jnp.bfloat16
F32 = jnp.float32
NN = (((1,), (0,)), ((), ()))
NTRANS = (((1,), (1,)), ((), ()))


def dot(left, right, dims=NN):
    return lax.dot_general(left, right, dims, preferred_element_type=F32)


def flip(index, bit):
    unit = 1 << bit
    own = lax.rem(index // unit, 2)
    return own, index + (1 - 2 * own) * unit


class Links:
    def __init__(self, row_bits):
        seq, row = lax.axis_index("seq"), lax.axis_index("rows")
        self.seq, self.row = seq, row
        self.core, other = flip(seq, 0)
        self.other_core = (other, row)
        x_bit, x_other = flip(seq, 1)
        diagonal = flip(other, 1)[1]
        self.peers = [seq, other, x_other, diagonal]
        dims = [(x_bit, (x_other, row))]
        for bit in range(row_bits):
            own, partner = flip(row, bit)
            dims.append((own, (seq, partner)))
        self.halving = dims[:3]
        self.extra = dims[3:]
        n = len(self.halving)
        orders = [(0, 1, 2), (1, 2, 0), (2, 0, 1)]
        self.orders = [[d for d in order if d < n] for order in orders]

    def all(self):
        return [self.other_core] + [p for _, p in self.halving + self.extra]

    def greet(self):
        barrier = pltpu.get_barrier_semaphore()
        whom = self.all() + [(self.peers[3], self.row)]
        for partner in whom:
            pl.semaphore_signal(barrier, inc=1, device_id=partner, device_id_type=MESH)
        pl.semaphore_wait(barrier, len(whom))


class Reducer:
    def __init__(self, links, grads, landing, small, send, recv, free):
        self.l, self.g, self.landing, self.small = links, grads, landing, small
        self.send, self.recv, self.free = send, recv, free
        n, e = len(links.halving), len(links.extra)
        self.n, self.e = n, e

    def span(self, t, level):
        low = 0
        for k in range(level):
            low = low + self.l.halving[self.l.orders[t][k]][0] * (PIECE >> (k + 1))
        return low if level == 0 else pl.multiple_of(low, 16)

    def copies(self, c, stage):
        l, n, e = self.l, self.n, self.e
        core, slot = l.core, lax.rem(c, SLOTS)
        if stage == 0:
            dst = self.landing.at[slot, :, pl.ds(0, PIECE)]
            return [self.make(self.g.at[c, :, 1 - core], dst, c, stage, 0, l.other_core)]
        if stage <= n:
            out = []
            for t in range(NT):
                own, partner = l.halving[l.orders[t][stage - 1]]
                rows = PIECE >> stage
                low = pl.multiple_of(self.span(t, stage - 1) + (1 - own) * rows, 16)
                src = self.g.at[c, t, core, pl.ds(low, rows)]
                dst = self.landing.at[slot, t, pl.ds(2 * PIECE - 2 * rows, rows)]
                out.append(self.make(src, dst, c, stage, t, partner))
            return out
        rows = PIECE >> n
        if stage <= n + e:
            partner = l.extra[stage - n - 1][1]
            out = []
            for t in range(NT):
                src = self.g.at[c, t, core, pl.ds(self.span(t, n), rows)]
                out.append(self.make(src, self.small.at[slot, stage - n - 1, t], c, stage, t, partner))
            return out
        k = 2 * n + e + 1 - stage
        if k > 0:
            out = []
            for t in range(NT):
                view = self.g.at[c, t, core, pl.ds(self.span(t, k), PIECE >> k)]
                out.append(self.make(view, view, c, stage, t, l.halving[l.orders[t][k - 1]][1]))
            return out
        view = self.g.at[c, :, core]
        return [self.make(view, view, c, stage, 0, l.other_core)]

    def make(self, src, dst, c, stage, t, partner):
        slot = lax.rem(c, SLOTS)
        return pltpu.make_async_remote_copy(
            src_ref=src, dst_ref=dst, send_sem=self.send.at[slot, stage, t], recv_sem=self.recv.at[slot, stage, t],
            device_id=partner, device_id_type=MESH)

    def fold(self, c, stage):
        n, e = self.n, self.e
        if stage > n + e:
            return
        core, slot = self.l.core, lax.rem(c, SLOTS)
        rows = PIECE >> min(stage, n)
        for t in range(NT):
            view = self.g.at[c, t, core, pl.ds(self.span(t, min(stage, n)), rows)]
            if stage <= n:
                got = self.landing[slot, t, pl.ds(0 if stage == 0 else 2 * PIECE - 2 * rows, rows)]
            else:
                got = self.small[slot, stage - n - 1, t]
            view[...] = view[...] + got

    def partners(self, level):
        if level == 0:
            return [(0, self.l.other_core)]
        return [(t, self.l.halving[self.l.orders[t][level - 1]][1]) for t in range(NT)]

    def shrink(self, k, c):
        if k > 0:
            for copy in self.copies(c, k - 1):
                copy.wait()
            self.fold(c, k - 1)
            if k - 1 <= self.n:
                for t, partner in self.partners(k - 1):
                    pl.semaphore_signal(self.free.at[k - 1, t], inc=1, device_id=partner, device_id_type=MESH)
        if k <= self.n + self.e:
            for copy in self.copies(c, k):
                copy.start()

    def spread(self, j, c):
        stage = self.n + self.e + 1 + j
        if j > 0:
            for copy in self.copies(c, stage - 1):
                copy.wait()
        if j <= self.n:
            for t, _ in self.partners(self.n - j):
                pl.semaphore_wait(self.free.at[self.n - j, t], 1)
            for copy in self.copies(c, stage):
                copy.start()

    def shrink_round(self, u, plan):
        for k in reversed(range(self.n + self.e + 2)):
            c, valid = plan(u - GAP * k)
            pl.when(valid)(partial(self.shrink, k, c))

    def spread_round(self, u, plan):
        for j in reversed(range(self.n + 2)):
            c, valid = plan(u - GAP * j)
            pl.when(valid)(partial(self.spread, j, c))


def reducer_scratch(row_bits):
    n, e = min(3, row_bits + 1), max(0, row_bits - 2)
    stages = 2 + 2 * n + e
    return [
        pltpu.VMEM((SLOTS, NT, 2 * PIECE - (PIECE >> n), 128), BF),
        pltpu.VMEM((SLOTS, max(e, 1), NT, PIECE >> n, 128), BF),
        pltpu.SemaphoreType.DMA((SLOTS, stages, NT)),
        pltpu.SemaphoreType.DMA((SLOTS, stages, NT)),
        pltpu.SemaphoreType.REGULAR((n + 1, NT)),
    ]


def half_of(pair, which):
    lane = lax.broadcasted_iota(jnp.int32, pair.shape, 1)
    return jnp.where((lane // HEAD_DIM) == which, pair, jnp.zeros_like(pair))


def inverse_rms(value):
    return lax.rsqrt(jnp.mean(value * value, axis=-1, keepdims=True) + EPSILON)


def layer_kernel(
    row_bits, sizes,
    blocks, ids, cotangent, w_q_hbm, w_k_hbm, w_v_hbm, w_out_hbm, gain_one, gain_two, w_gate, w_up, w_down,
    y_back, dx_back, grads, gain_sums,
    x_in, g_in, id_rows, id_q, id_k, n1_t, q, k, v, o_t, lse, x_one, n2, n2_t, acc, d_one, sent, d_both, h_low, w_qkv, w_out, both_buf, down_buf,
    dk_acc, dv_acc, gains, gains_in,
    landing, small, send, recv, free,
    w_sem, ff_sem, own_sem, row_send, row_recv, gain_send, gain_recv,
):
    tokens, positions, features, hidden, heads = sizes
    ff_chunks, groups, pairs = hidden // COLS, features // COLS, heads // 2
    count = tokens // positions
    out_chunk = ff_chunks
    chunks = ff_chunks + 1 + groups
    scale = HEAD_DIM ** (-0.5)
    scale_two = scale * 1.4426950408889634
    links = Links(row_bits)
    seq, row = links.seq, links.row
    reducer = Reducer(links, grads, landing, small, send, recv, free)

    def tile_of(d):
        return slice(positions * d, positions * (d + 1))

    def part_of(ref, d):
        return ref.at[pl.ds(positions * d, positions)]

    loads = [pltpu.make_async_copy(w, w_qkv.at[i], w_sem.at[i]) for i, w in enumerate((w_q_hbm, w_k_hbm, w_v_hbm))]
    loads.append(pltpu.make_async_copy(w_out_hbm, w_out, w_sem.at[3]))
    own = [
        pltpu.make_async_copy(blocks.at[seq], part_of(x_in, 0), own_sem.at[0]),
        pltpu.make_async_copy(ids, id_rows.at[0], own_sem.at[1]),
        pltpu.make_async_copy(cotangent.at[seq], part_of(g_in, 0), own_sem.at[2]),
    ]
    own[0].start()
    for copy in loads:
        copy.start()
    own[1].start()
    own[2].start()
    links.greet()

    def to_peer(a, d, src, dst):
        return pltpu.make_async_remote_copy(
            src_ref=src, dst_ref=dst, send_sem=row_send.at[a, d], recv_sem=row_recv.at[a, d],
            device_id=(links.peers[d], row), device_id_type=MESH)

    x_moves = [to_peer(0, d, blocks.at[links.peers[d]], part_of(x_in, d)) for d in range(1, count)]
    id_moves = [to_peer(1, d, ids, id_rows.at[d]) for d in range(1, count)]
    g_moves = [to_peer(2, d, cotangent.at[links.peers[d]], part_of(g_in, d)) for d in range(1, count)]
    for copy in id_moves + x_moves + g_moves:
        copy.start()

    def project(d):
        tile = tile_of(d)
        value = x_in[tile, :].astype(F32)
        normed = (value * inverse_rms(value) * gain_one[...].reshape(1, features)).astype(BF)
        n1_t[:, tile] = normed.T
        for i, made in enumerate((q, k, v)):
            made[tile, :] = dot(normed, w_qkv[i]).astype(BF)

    own[0].wait()
    for copy in loads[:3]:
        copy.wait()
    project(0)
    x_moves[0].wait()
    project(1)

    own[1].wait()
    for copy in id_moves:
        copy.wait()
    for d in range(count):
        id_q[0:1, tile_of(d)] = id_rows[d, pl.ds(seq, 1), :]
    for j in range(tokens // 128):
        block = jnp.broadcast_to(id_q[0:1, 128 * j : 128 * j + 128], (128, 128))
        id_k[128 * j : 128 * j + 128, :] = block.T

    def scores_of(key, keys, queries, cols):
        width = queries.stop - queries.start
        scores = dot(key, q[queries, cols], NTRANS) * scale_two
        same = jnp.concatenate([id_k[keys, :]] * (width // 128), axis=1) == id_q[0:1, queries]
        return jnp.where(same, scores, MASKED)

    o_part = d_one

    def attend(blocks, p, _):
        cols = pl.ds(pl.multiple_of(p * 128, 128), 128)
        used = slice(0, max(keys.stop for keys, _, _, _ in blocks))
        key_pair = k[used, cols]
        value_t = v[used, cols].T
        sides = [half_of(key_pair, h) for h in range(2)]
        work = [(h,) + block for block in blocks for h in range(2)]

        def score(h, keys, queries, joined, final):
            return scores_of(sides[h][keys], keys, queries, cols)

        def weigh(scores, h, keys, queries, joined, final):
            at = p * 2 + h
            largest = jnp.max(scores, axis=0, keepdims=True)
            kept = None
            if joined:
                before = lse[at, 0:1, queries]
                largest = jnp.maximum(before, largest)
                kept = jnp.exp2(before - largest)
            exponent = jnp.exp2(scores - largest)
            total = jnp.sum(exponent, axis=0, keepdims=True)
            if joined:
                total += lse[at, 1:2, queries] * kept
            if final:
                lse[at, 0:1, queries] = largest + jnp.log2(total)
            else:
                lse[at, 0:1, queries] = largest
                lse[at, 1:2, queries] = total
            return exponent.astype(BF), total, kept

        def mix(weights, h, keys, queries, joined, final):
            exponent, total, kept = weights
            rows = pl.ds(pl.multiple_of(p * 128 + HEAD_DIM * h, HEAD_DIM), HEAD_DIM)
            mixed = dot(value_t[HEAD_DIM * h : HEAD_DIM * (h + 1), keys], exponent)
            if joined:
                mixed += o_part[rows, queries] * kept
            if final:
                o_t[rows, queries] = (mixed / total).astype(BF)
            else:
                o_part[rows, queries] = mixed

        scores, behind = score(*work[0]), None
        for i, block in enumerate(work):
            ahead = score(*work[i + 1]) if i + 1 < len(work) else None
            weights = weigh(scores, *block)
            if behind is not None:
                mix(behind[0], *behind[1])
            scores, behind = ahead, (weights, block)
        mix(behind[0], *behind[1])
        return 0

    ends = [positions * d for d in range(count + 1)]
    lax.fori_loop(0, pairs, partial(attend, [(slice(0, ends[2]), slice(0, ends[2]), False, False)]), 0)
    x_moves[1].wait()
    project(2)
    third, fourth = slice(ends[2], ends[3]), slice(ends[3], ends[4])
    lax.fori_loop(0, pairs, partial(attend, [
        (slice(0, ends[3]), third, False, False), (third, slice(0, ends[2]), True, False)]), 0)
    x_moves[2].wait()
    project(3)
    lax.fori_loop(0, pairs, partial(attend, [
        (slice(0, ends[4]), fourth, False, True), (fourth, slice(0, ends[3]), True, True)]), 0)

    def ff_loads(c):
        slot = lax.rem(c, 2)
        cols = pl.ds(pl.multiple_of(c * COLS, COLS), COLS)
        return [
            pltpu.make_async_copy(w_gate.at[:, cols], both_buf.at[slot, :, pl.ds(0, COLS)], ff_sem.at[slot, 0]),
            pltpu.make_async_copy(w_up.at[:, cols], both_buf.at[slot, :, pl.ds(COLS, COLS)], ff_sem.at[slot, 1]),
            pltpu.make_async_copy(w_down.at[cols, :], down_buf.at[slot], ff_sem.at[slot, 2]),
        ]

    for copy in ff_loads(0):
        copy.start()

    loads[3].wait()

    def project_tile(i, _):
        tile = pl.ds(pl.multiple_of(i * positions, positions), positions)
        mixed = o_t[:, tile].T
        value = x_in[tile, :].astype(F32) + dot(mixed, w_out[...])
        normed = (value * inverse_rms(value) * gain_two[...].reshape(1, features)).astype(BF)
        x_one[tile, :] = value
        acc[tile, :] = value
        n2[tile, :] = normed
        n2_t[:, tile] = normed.T
        d_one[tile, :] = jnp.zeros((positions, features), F32)
        return 0

    lax.fori_loop(0, count, project_tile, 0)
    own[2].wait()
    for copy in g_moves:
        copy.wait()

    down = reducer.n + reducer.e + 1
    late_down = out_chunk + 4

    def shrink_plan(u):
        late = u - late_down
        chunk = jnp.where(u <= out_chunk, u, out_chunk + 1 + late // 4)
        valid = (u >= 0) & ((u <= out_chunk) | ((late >= 0) & (late <= 4 * (groups - 1)) & (lax.rem(late, 4) == 0)))
        return chunk, valid

    def spread_plan(u):
        return shrink_plan(u - GAP * down)

    def advance(u):
        reducer.shrink_round(u, shrink_plan)
        reducer.spread_round(u, spread_plan)

    def put(c, t, piece):
        for half in range(2):
            grads[c, t, half] = piece[:, 128 * half : 128 * half + 128].astype(BF)

    half_tokens = tokens // 2

    def ff_chunk(c, _):
        slot = lax.rem(c, 2)

        @pl.when(c + 1 < ff_chunks)
        def _():
            for copy in ff_loads(c + 1):
                copy.start()

        for copy in ff_loads(c):
            copy.wait()
        for i in range(2):
            tile = slice(half_tokens * i, half_tokens * (i + 1))
            both = dot(n2[tile, :], both_buf[slot])
            gate, up = both[:, :COLS], both[:, COLS:]
            d_hidden = dot(g_in[tile, :], down_buf[slot], NTRANS)
            square = gate * gate
            bend = 0.7978845608028654 * 0.044715
            turn = jnp.tanh(gate * (0.7978845608028654 + bend * square))
            rise = 0.5 + 0.5 * turn
            activated = gate * rise
            slope = rise + 0.5 * gate * (1.0 - turn * turn) * (0.7978845608028654 + 3.0 * bend * square)
            low_h = (activated * up).astype(BF)
            low_both = jnp.concatenate([(d_hidden * up * slope).astype(BF), (d_hidden * activated).astype(BF)], axis=1)
            d_both[tile, :] = low_both
            h_low[tile, :] = low_h
            acc[tile, :] += dot(low_h, down_buf[slot])
            d_one[tile, :] += dot(low_both, both_buf[slot], NTRANS)
        made = dot(n2_t[...], d_both[...])
        put(c, 0, made[:, :COLS])
        put(c, 1, made[:, COLS:])
        made = dot(h_low[...].T, g_in[...])
        for j in range(NT):
            for half in range(2):
                at = COLS * j + 128 * half
                grads[c, 2, half, COLS * j : COLS * (j + 1), :] = made[:, at : at + 128].astype(BF)
        reducer.shrink_round(c, shrink_plan)
        return 0

    lax.fori_loop(0, ff_chunks, ff_chunk, 0)

    gains[...] = jnp.zeros_like(gains)
    for d in range(count):
        tile = tile_of(d)
        sent[tile, :] = acc[tile, :].astype(BF)

    def whole_back(a, dst):
        own_copy = pltpu.make_async_copy(part_of(sent, 0), dst.at[seq], own_sem.at[a])
        return [own_copy] + [to_peer(a, d, part_of(sent, d), dst.at[seq]) for d in range(1, count)]

    def piece_back(a, dst, i, pieces):
        rows = positions // pieces
        for d in range(2, count):
            low = pl.multiple_of(positions * d + i * rows, 16)
            to = pl.ds(pl.multiple_of(i * rows, 16), rows)
            to_peer(a, d, sent.at[pl.ds(low, rows)], dst.at[seq, to]).start()

    y_moves = whole_back(0, y_back)
    for copy in y_moves[:2]:
        copy.start()
    for d in range(count):
        tile = tile_of(d)
        value = x_one[tile, :]
        inverse = inverse_rms(value)
        slope = d_one[tile, :]
        hat = value * inverse
        gains[1:2, :] += jnp.sum(slope * hat, axis=0, keepdims=True)
        weighted = slope * gain_two[...].reshape(1, features)
        pulled = inverse * (weighted - hat * jnp.mean(weighted * hat, axis=-1, keepdims=True))
        total = g_in[tile, :].astype(F32) + pulled
        d_one[tile, :] = total
        low = total.astype(BF)
        g_in[tile, :] = low
        d_mixed = dot(low, w_out[...], NTRANS).astype(BF)
        n2[tile, :] = d_mixed
        n2_t[:, tile] = d_mixed.T
    for t in range(NT):
        put(out_chunk, t, dot(o_t[...], g_in[:, COLS * t : COLS * (t + 1)]))
    reducer.shrink_round(jnp.int32(out_chunk), shrink_plan)

    width = 256

    def backward_pair(step, _):
        g, j = step // 2, lax.rem(step, 2)
        cols = pl.ds(pl.multiple_of(step * 128, 128), 128)
        key_pair, value_pair = k[:, cols], v[:, cols]
        key_t = key_pair.T
        dq = []
        for h in range(2):
            key, value = half_of(key_pair, h), half_of(value_pair, h)
            rows = pl.ds(pl.multiple_of(step * 128 + HEAD_DIM * h, HEAD_DIM), HEAD_DIM)
            dq_parts = []
            for i in range(tokens // width):
                qs = slice(width * i, width * (i + 1))
                scores = scores_of(key, slice(0, tokens), qs, cols)
                prob = jnp.exp2(scores - lse[step * 2 + h, 0:1, qs])
                delta = jnp.sum(n2_t[rows, qs].astype(F32) * o_t[rows, qs].astype(F32), axis=0, keepdims=True)
                d_prob = dot(value, n2[qs, cols], NTRANS)
                d_score = (prob * (d_prob - delta)).astype(BF)
                low = prob.astype(BF)
                dv = dot(low, n2[qs, cols])
                dk = dot(d_score, q[qs, cols])
                if i == 0:
                    dv_acc[h] = dv
                    dk_acc[h] = dk
                else:
                    dv_acc[h] += dv
                    dk_acc[h] += dk
                dq_parts.append((dot(key_t[HEAD_DIM * h : HEAD_DIM * (h + 1)], d_score) * scale).astype(BF))
            dq.append(jnp.concatenate(dq_parts, axis=1))
            if h == 0:
                advance(out_chunk + 1 + 2 * step)

                @pl.when(step < Y_PIECES // 2)
                def _():
                    piece_back(0, y_back, 2 * step, Y_PIECES)
        lane = lax.broadcasted_iota(jnp.int32, (tokens, 128), 1) < HEAD_DIM
        q[:, cols] = jnp.concatenate(dq, axis=0).T
        k[:, cols] = (jnp.where(lane, dk_acc[0], dk_acc[1]) * scale).astype(BF)
        v[:, cols] = jnp.where(lane, dv_acc[0], dv_acc[1]).astype(BF)

        @pl.when(j == 1)
        def _():
            group = pl.ds(pl.multiple_of(g * COLS, COLS), COLS)
            for t, made in enumerate((q, k, v)):
                put(out_chunk + 1 + g, t, dot(n1_t[...], made[:, group]))

        advance(out_chunk + 2 + 2 * step)

        @pl.when(step < Y_PIECES // 2)
        def _():
            piece_back(0, y_back, 2 * step + 1, Y_PIECES)

        return 0

    lax.fori_loop(0, pairs, backward_pair, 0)

    for copy in y_moves:
        copy.wait()
    dx_moves = whole_back(1, dx_back)
    for d in reversed(range(count)):
        tile = tile_of(d)
        slope = sum(dot(made[tile, :], w_qkv[t], NTRANS) for t, made in enumerate((q, k, v)))
        value = x_in[tile, :].astype(F32)
        inverse = inverse_rms(value)
        hat = value * inverse
        gains[0:1, :] += jnp.sum(slope * hat, axis=0, keepdims=True)
        weighted = slope * gain_one[...].reshape(1, features)
        pulled = inverse * (weighted - hat * jnp.mean(weighted * hat, axis=-1, keepdims=True))
        sent[tile, :] = (d_one[tile, :] + pulled).astype(BF)
    for copy in dx_moves[:2]:
        copy.start()

    axes = links.all()

    def gain_copy(i):
        return pltpu.make_async_remote_copy(
            src_ref=gains, dst_ref=gains_in.at[i], send_sem=gain_send.at[i], recv_sem=gain_recv.at[i],
            device_id=axes[i], device_id_type=MESH)

    begin = out_chunk + 1 + 2 * pairs
    last = late_down + 4 * (groups - 1) + GAP * (down + reducer.n + 1)

    def tail(r, _):
        for i in range(len(axes) + 1):

            @pl.when(r == begin + i)
            def _():
                if i > 0:
                    gain_copy(i - 1).wait()
                    gains[...] += gains_in[i - 1]
                if i < len(axes):
                    gain_copy(i).start()

        advance(r)

        @pl.when(r < begin + X_PIECES)
        def _():
            piece_back(1, dx_back, r - begin, X_PIECES)

        return 0

    lax.fori_loop(begin, max(last + 1, begin + max(len(axes) + 1, X_PIECES)), tail, 0)
    gain_sums[...] = gains[...]
    for copy in dx_moves:
        copy.wait()


def run_layer(row_bits, blocks, ids, cotangent, w_query, w_key, w_value, w_out, gain_one, gain_two, w_gate, w_up, w_down):
    count, positions, features = blocks.shape
    hidden = w_gate.shape[1]
    tokens, heads = count * positions, features // HEAD_DIM
    chunks = hidden // COLS + 1 + features // COLS
    axes = row_bits + 2
    sizes = (tokens, positions, features, hidden, heads)
    anywhere, inside = pl.BlockSpec(memory_space=pl.ANY), pl.BlockSpec(memory_space=pltpu.VMEM)
    back = jax.ShapeDtypeStruct(blocks.shape, BF)
    low = pltpu.VMEM((tokens, features), BF)
    turned = pltpu.VMEM((features, tokens), BF)
    full = pltpu.VMEM((tokens, features), F32)
    dma = pltpu.SemaphoreType.DMA
    return pl.pallas_call(
        partial(layer_kernel, row_bits, sizes),
        out_shape=(back, back, pltpu.VMEM((chunks, NT, 2, PIECE, 128), BF), jax.ShapeDtypeStruct((8, features), F32)),
        in_specs=[anywhere] * 7 + [inside] * 2 + [anywhere] * 3,
        out_specs=[anywhere] * 2 + [inside] * 2,
        scratch_shapes=[
            low, low,
            pltpu.VMEM((count, count, positions), jnp.int32), pltpu.VMEM((8, tokens), jnp.int32), pltpu.VMEM((tokens, 128), jnp.int32),
            turned, low, low, low, turned, pltpu.VMEM((heads, 8, tokens), F32), full, low, turned, full, full, low,
            pltpu.VMEM((tokens, 2 * COLS), BF), pltpu.VMEM((tokens, COLS), BF),
            pltpu.VMEM((3, features, features), BF), pltpu.VMEM((features, features), BF),
            pltpu.VMEM((2, features, 2 * COLS), BF), pltpu.VMEM((2, COLS, features), BF),
            pltpu.VMEM((2, tokens, 128), F32), pltpu.VMEM((2, tokens, 128), F32),
            pltpu.VMEM((8, features), F32), pltpu.VMEM((axes, 8, features), F32),
        ] + reducer_scratch(row_bits) + [
            dma((4,)), dma((2, 3)), dma((3,)), dma((3, count)), dma((3, count)), dma((axes,)), dma((axes,)),
        ],
        compiler_params=pltpu.CompilerParams(collective_id=0, has_side_effects=True, vmem_limit_bytes=49 * 2**20),
        cost_estimate=pl.CostEstimate(flops=60 * 10**9, bytes_accessed=60 * 10**6, transcendentals=10**7),
    )(blocks, ids, cotangent, w_query, w_key, w_value, w_out, gain_one, gain_two, w_gate, w_up, w_down)


def widen_kernel(
    ff_chunks, groups,
    low, y_in, dx_in, gain_sums,
    y, dx, g_q, g_k, g_v, g_out, g_one, g_two, g_gate, g_up, g_down,
    wide, wide_down, held, out_sem, move_sem,
):
    chunks = ff_chunks + 1 + groups
    arrive = [pltpu.make_async_copy(src, held.at[i], move_sem.at[0, i]) for i, src in enumerate((y_in, dx_in))]
    leave = [pltpu.make_async_copy(held.at[i], dst, move_sem.at[1, i]) for i, dst in enumerate((y, dx))]

    def stores(c):
        slot = c % 2
        cols = pl.ds(COLS * c, COLS)
        if c < ff_chunks:
            pairs = [(wide.at[slot, 0], g_gate.at[:, cols]), (wide.at[slot, 1], g_up.at[:, cols]), (wide_down.at[slot], g_down.at[cols, :])]
        elif c == ff_chunks:
            pairs = [(wide.at[slot, t], g_out.at[:, pl.ds(COLS * t, COLS)]) for t in range(NT)]
        else:
            cols = pl.ds(COLS * (c - ff_chunks - 1), COLS)
            pairs = [(wide.at[slot, t], made.at[:, cols]) for t, made in enumerate((g_q, g_k, g_v))]
        return [pltpu.make_async_copy(src, dst, out_sem.at[slot, t]) for t, (src, dst) in enumerate(pairs)]

    for copy in arrive:
        copy.start()
    g_one[...] = gain_sums[0, :]
    g_two[...] = gain_sums[1, :]
    for c in range(chunks):
        if c >= 2:
            for copy in stores(c - 2):
                copy.wait()
        for half in range(2):
            cols = slice(128 * half, 128 * half + 128)
            for t in range(NT):
                if t == 2 and c < ff_chunks:
                    for j in range(NT):
                        at = COLS * j + 128 * half
                        wide_down[c % 2, :, at : at + 128] = low[c, t, half, COLS * j : COLS * (j + 1), :].astype(F32)
                else:
                    wide[c % 2, t, :, cols] = low[c, t, half].astype(F32)
        for copy in stores(c):
            copy.start()
        if c < 2:
            arrive[c].wait()
            leave[c].start()
    for c in range(chunks - 2, chunks):
        for copy in stores(c):
            copy.wait()
    for copy in leave:
        copy.wait()


def widen(summed, y, dx, gains, features, hidden):
    anywhere, inside = pl.BlockSpec(memory_space=pl.ANY), pl.BlockSpec(memory_space=pltpu.VMEM)
    square, gain = jax.ShapeDtypeStruct((features, features), F32), jax.ShapeDtypeStruct((features,), F32)
    flat, tall = jax.ShapeDtypeStruct((features, hidden), F32), jax.ShapeDtypeStruct((hidden, features), F32)
    back = jax.ShapeDtypeStruct(y.shape, y.dtype)
    dma = pltpu.SemaphoreType.DMA
    return pl.pallas_call(
        partial(widen_kernel, hidden // COLS, features // COLS),
        out_shape=(back, back) + (square,) * 4 + (gain,) * 2 + (flat, flat, tall),
        in_specs=[inside] + [pl.BlockSpec(memory_space=pltpu.HBM)] * 2 + [inside],
        out_specs=[anywhere] * 6 + [inside] * 2 + [anywhere] * 3,
        scratch_shapes=[
            pltpu.VMEM((2, NT, PIECE, COLS), F32), pltpu.VMEM((2, COLS, features), F32), pltpu.VMEM((2,) + y.shape, BF),
            dma((2, NT)), dma((2, 2)),
        ],
        compiler_params=pltpu.CompilerParams(vmem_limit_bytes=48 * 2**20),
    )(pltpu.with_memory_space_constraint(summed, pltpu.VMEM), y, dx, gains)


def body(row_bits, blocks, segment_ids, cotangent, w_query, w_key, w_value, w_out, norm_one, norm_two, w_gate, w_up, w_down):
    features, hidden = w_gate.shape
    y, dx, summed, gains = run_layer(
        row_bits, blocks, segment_ids, cotangent, w_query, w_key, w_value, w_out, norm_one, norm_two, w_gate, w_up, w_down)
    return widen(summed, y, dx, gains, features, hidden)


def solution(mesh):
    split = P("rows", "seq", None)
    row_bits = (mesh.shape["rows"] - 1).bit_length()
    return jax.shard_map(
        partial(body, row_bits),
        mesh=mesh,
        in_specs=(split, P("rows", "seq"), split) + (P(),) * 9,
        out_specs=(split, split) + (P(),) * 9,
        check_vma=False,
    )
```

```python
from functools import partial

import jax
import jax.numpy as jnp
from jax import lax
from jax.experimental import pallas as pl
from jax.experimental.pallas import tpu as pltpu
from jax.sharding import PartitionSpec as P

MESH = pl.DeviceIdType.MESH
HEAD_DIM = 64
EPSILON = 1e-06
MASKED = -1000000000.0
PIECE = 768
NT = 3
COLS = 256
SLOTS = 4
GAP = 2
Y_PIECES = 8
X_PIECES = 16
BF = jnp.bfloat16
F32 = jnp.float32
NN = (((1,), (0,)), ((), ()))
NTRANS = (((1,), (1,)), ((), ()))


def dot(left, right, dims=NN):
    return lax.dot_general(left, right, dims, preferred_element_type=F32)


def flip(index, bit):
    unit = 1 << bit
    own = lax.rem(index // unit, 2)
    return own, index + (1 - 2 * own) * unit


class Links:
    def __init__(self, row_bits):
        seq, row = lax.axis_index("seq"), lax.axis_index("rows")
        self.seq, self.row = seq, row
        self.core, other = flip(seq, 0)
        self.other_core = (other, row)
        x_bit, x_other = flip(seq, 1)
        diagonal = flip(other, 1)[1]
        self.peers = [seq, other, x_other, diagonal]
        dims = [(x_bit, (x_other, row))]
        for bit in range(row_bits):
            own, partner = flip(row, bit)
            dims.append((own, (seq, partner)))
        self.halving = dims[:3]
        self.extra = dims[3:]
        n = len(self.halving)
        orders = [(0, 1, 2), (1, 2, 0), (2, 0, 1)]
        others = [(1, 0, 2), (1, 2, 0), (2, 0, 1)]
        self.orders = [[[d for d in order if d < n] for order in both] for both in (orders, others)]

    def level(self, c, t, k):
        here, there = (both[t][k] for both in self.orders)
        if here == there:
            return self.halving[here]
        even = 1 - lax.rem(c, 2)
        (own_a, (seq_a, row_a)), (own_b, (seq_b, row_b)) = self.halving[here], self.halving[there]
        pick = lambda a, b: a + (b - a) * even
        return pick(own_a, own_b), (pick(seq_a, seq_b), pick(row_a, row_b))

    def all(self):
        return [self.other_core] + [p for _, p in self.halving + self.extra]

    def greet(self):
        barrier = pltpu.get_barrier_semaphore()
        whom = self.all() + [(self.peers[3], self.row)]
        for partner in whom:
            pl.semaphore_signal(barrier, inc=1, device_id=partner, device_id_type=MESH)
        pl.semaphore_wait(barrier, len(whom))


class Reducer:
    def __init__(self, links, grads, landing, small, send, recv, free):
        self.l, self.g, self.landing, self.small = links, grads, landing, small
        self.send, self.recv, self.free = send, recv, free
        n, e = len(links.halving), len(links.extra)
        self.n, self.e = n, e

    def span(self, c, t, level):
        low = 0
        for k in range(level):
            low = low + self.l.level(c, t, k)[0] * (PIECE >> (k + 1))
        return low if level == 0 else pl.multiple_of(low, 16)

    def copies(self, c, stage):
        l, n, e = self.l, self.n, self.e
        core, slot = l.core, lax.rem(c, SLOTS)
        if stage == 0:
            dst = self.landing.at[slot, :, pl.ds(0, PIECE)]
            return [self.make(self.g.at[c, :, 1 - core], dst, c, stage, 0, l.other_core)]
        if stage <= n:
            out = []
            for t in range(NT):
                own, partner = l.level(c, t, stage - 1)
                rows = PIECE >> stage
                low = pl.multiple_of(self.span(c, t, stage - 1) + (1 - own) * rows, 16)
                src = self.g.at[c, t, core, pl.ds(low, rows)]
                dst = self.landing.at[slot, t, pl.ds(2 * PIECE - 2 * rows, rows)]
                out.append(self.make(src, dst, c, stage, t, partner))
            return out
        rows = PIECE >> n
        if stage <= n + e:
            partner = l.extra[stage - n - 1][1]
            out = []
            for t in range(NT):
                src = self.g.at[c, t, core, pl.ds(self.span(c, t, n), rows)]
                out.append(self.make(src, self.small.at[slot, stage - n - 1, t], c, stage, t, partner))
            return out
        k = 2 * n + e + 1 - stage
        if k > 0:
            out = []
            for t in range(NT):
                view = self.g.at[c, t, core, pl.ds(self.span(c, t, k), PIECE >> k)]
                out.append(self.make(view, view, c, stage, t, l.level(c, t, k - 1)[1]))
            return out
        view = self.g.at[c, :, core]
        return [self.make(view, view, c, stage, 0, l.other_core)]

    def make(self, src, dst, c, stage, t, partner):
        slot = lax.rem(c, SLOTS)
        return pltpu.make_async_remote_copy(
            src_ref=src, dst_ref=dst, send_sem=self.send.at[slot, stage, t], recv_sem=self.recv.at[slot, stage, t],
            device_id=partner, device_id_type=MESH)

    def fold(self, c, stage):
        n, e = self.n, self.e
        if stage > n + e:
            return
        core, slot = self.l.core, lax.rem(c, SLOTS)
        rows = PIECE >> min(stage, n)
        for t in range(NT):
            view = self.g.at[c, t, core, pl.ds(self.span(c, t, min(stage, n)), rows)]
            if stage <= n:
                got = self.landing[slot, t, pl.ds(0 if stage == 0 else 2 * PIECE - 2 * rows, rows)]
            else:
                got = self.small[slot, stage - n - 1, t]
            view[...] = view[...] + got

    def partners(self, c, level):
        if level == 0:
            return [(0, self.l.other_core)]
        return [(t, self.l.level(c, t, level - 1)[1]) for t in range(NT)]

    def shrink(self, k, c):
        if k > 0:
            for copy in self.copies(c, k - 1):
                copy.wait()
            self.fold(c, k - 1)
            if k - 1 <= self.n:
                for t, partner in self.partners(c, k - 1):
                    pl.semaphore_signal(self.free.at[k - 1, t, lax.rem(c, 2)], inc=1, device_id=partner, device_id_type=MESH)
        if k <= self.n + self.e:
            for copy in self.copies(c, k):
                copy.start()

    def spread(self, j, c):
        stage = self.n + self.e + 1 + j
        if j > 0:
            for copy in self.copies(c, stage - 1):
                copy.wait()
        if j <= self.n:
            for t, _ in self.partners(c, self.n - j):
                pl.semaphore_wait(self.free.at[self.n - j, t, lax.rem(c, 2)], 1)
            for copy in self.copies(c, stage):
                copy.start()

    def shrink_round(self, u, plan):
        for k in reversed(range(self.n + self.e + 2)):
            c, valid = plan(u - GAP * k)
            pl.when(valid)(partial(self.shrink, k, c))

    def spread_round(self, u, plan):
        for j in reversed(range(self.n + 2)):
            c, valid = plan(u - GAP * j)
            pl.when(valid)(partial(self.spread, j, c))


def reducer_scratch(row_bits):
    n, e = min(3, row_bits + 1), max(0, row_bits - 2)
    stages = 2 + 2 * n + e
    return [
        pltpu.VMEM((SLOTS, NT, 2 * PIECE - (PIECE >> n), 128), BF),
        pltpu.VMEM((SLOTS, max(e, 1), NT, PIECE >> n, 128), BF),
        pltpu.SemaphoreType.DMA((SLOTS, stages, NT)),
        pltpu.SemaphoreType.DMA((SLOTS, stages, NT)),
        pltpu.SemaphoreType.REGULAR((n + 1, NT, 2)),
    ]


def half_of(pair, which):
    lane = lax.broadcasted_iota(jnp.int32, pair.shape, 1)
    return jnp.where((lane // HEAD_DIM) == which, pair, jnp.zeros_like(pair))


def inverse_rms(value):
    return lax.rsqrt(jnp.mean(value * value, axis=-1, keepdims=True) + EPSILON)


def layer_kernel(
    row_bits, sizes,
    blocks, ids, cotangent, w_q_hbm, w_k_hbm, w_v_hbm, w_out_hbm, gain_one, gain_two, w_gate, w_up, w_down,
    y_back, dx_back, grads, gain_sums,
    x_in, g_in, id_rows, id_q, id_k, n1_t, q, k, v, o_t, lse, x_one, n2, n2_t, acc, d_one, sent, d_both, h_low, w_qkv, w_out, both_buf, down_buf,
    dk_acc, dv_acc, gains, gains_in,
    landing, small, send, recv, free,
    w_sem, ff_sem, own_sem, row_send, row_recv, gain_send, gain_recv,
):
    tokens, positions, features, hidden, heads = sizes
    ff_chunks, groups, pairs = hidden // COLS, features // COLS, heads // 2
    count = tokens // positions
    out_chunk = ff_chunks
    chunks = ff_chunks + 1 + groups
    scale = HEAD_DIM ** (-0.5)
    scale_two = scale * 1.4426950408889634
    links = Links(row_bits)
    seq, row = links.seq, links.row
    reducer = Reducer(links, grads, landing, small, send, recv, free)

    def tile_of(d):
        return slice(positions * d, positions * (d + 1))

    def part_of(ref, d):
        return ref.at[pl.ds(positions * d, positions)]

    loads = [pltpu.make_async_copy(w, w_qkv.at[i], w_sem.at[i]) for i, w in enumerate((w_q_hbm, w_k_hbm, w_v_hbm))]
    loads.append(pltpu.make_async_copy(w_out_hbm, w_out, w_sem.at[3]))
    own = [
        pltpu.make_async_copy(blocks.at[seq], part_of(x_in, 0), own_sem.at[0]),
        pltpu.make_async_copy(ids, id_rows.at[0], own_sem.at[1]),
        pltpu.make_async_copy(cotangent.at[seq], part_of(g_in, 0), own_sem.at[2]),
    ]
    own[0].start()
    for copy in loads:
        copy.start()
    own[1].start()
    own[2].start()
    links.greet()

    def to_peer(a, d, src, dst):
        return pltpu.make_async_remote_copy(
            src_ref=src, dst_ref=dst, send_sem=row_send.at[a, d], recv_sem=row_recv.at[a, d],
            device_id=(links.peers[d], row), device_id_type=MESH)

    x_moves = [to_peer(0, d, blocks.at[links.peers[d]], part_of(x_in, d)) for d in range(1, count)]
    id_moves = [to_peer(1, d, ids, id_rows.at[d]) for d in range(1, count)]
    g_moves = [to_peer(2, d, cotangent.at[links.peers[d]], part_of(g_in, d)) for d in range(1, count)]
    for copy in id_moves + x_moves + g_moves:
        copy.start()

    def project(d):
        tile = tile_of(d)
        value = x_in[tile, :].astype(F32)
        normed = (value * inverse_rms(value) * gain_one[...].reshape(1, features)).astype(BF)
        n1_t[:, tile] = normed.T
        for i, made in enumerate((q, k, v)):
            made[tile, :] = dot(normed, w_qkv[i]).astype(BF)

    own[0].wait()
    for copy in loads[:3]:
        copy.wait()
    project(0)
    x_moves[0].wait()
    project(1)

    own[1].wait()
    for copy in id_moves:
        copy.wait()
    for d in range(count):
        id_q[0:1, tile_of(d)] = id_rows[d, pl.ds(seq, 1), :]
    for j in range(tokens // 128):
        block = jnp.broadcast_to(id_q[0:1, 128 * j : 128 * j + 128], (128, 128))
        id_k[128 * j : 128 * j + 128, :] = block.T

    def scores_of(key, keys, queries, cols):
        width = queries.stop - queries.start
        scores = dot(key, q[queries, cols], NTRANS) * scale_two
        same = jnp.concatenate([id_k[keys, :]] * (width // 128), axis=1) == id_q[0:1, queries]
        return jnp.where(same, scores, MASKED)

    o_part = d_one

    def attend(blocks, p, _):
        cols = pl.ds(pl.multiple_of(p * 128, 128), 128)
        used = slice(0, max(keys.stop for keys, _, _, _ in blocks))
        key_pair = k[used, cols]
        value_t = v[used, cols].T
        sides = [half_of(key_pair, h) for h in range(2)]
        work = [(h,) + block for block in blocks for h in range(2)]

        def score(h, keys, queries, joined, final):
            return scores_of(sides[h][keys], keys, queries, cols)

        def weigh(scores, h, keys, queries, joined, final):
            at = p * 2 + h
            largest = jnp.max(scores, axis=0, keepdims=True)
            kept = None
            if joined:
                before = lse[at, 0:1, queries]
                largest = jnp.maximum(before, largest)
                kept = jnp.exp2(before - largest)
            exponent = jnp.exp2(scores - largest)
            total = jnp.sum(exponent, axis=0, keepdims=True)
            if joined:
                total += lse[at, 1:2, queries] * kept
            if final:
                lse[at, 0:1, queries] = largest + jnp.log2(total)
            else:
                lse[at, 0:1, queries] = largest
                lse[at, 1:2, queries] = total
            return exponent.astype(BF), total, kept

        def mix(weights, h, keys, queries, joined, final):
            exponent, total, kept = weights
            rows = pl.ds(pl.multiple_of(p * 128 + HEAD_DIM * h, HEAD_DIM), HEAD_DIM)
            mixed = dot(value_t[HEAD_DIM * h : HEAD_DIM * (h + 1), keys], exponent)
            if joined:
                mixed += o_part[rows, queries] * kept
            if final:
                o_t[rows, queries] = (mixed / total).astype(BF)
            else:
                o_part[rows, queries] = mixed

        scores, behind = score(*work[0]), None
        for i, block in enumerate(work):
            ahead = score(*work[i + 1]) if i + 1 < len(work) else None
            weights = weigh(scores, *block)
            if behind is not None:
                mix(behind[0], *behind[1])
            scores, behind = ahead, (weights, block)
        mix(behind[0], *behind[1])
        return 0

    ends = [positions * d for d in range(count + 1)]
    lax.fori_loop(0, pairs, partial(attend, [(slice(0, ends[2]), slice(0, ends[2]), False, False)]), 0)
    x_moves[1].wait()
    project(2)
    third, fourth = slice(ends[2], ends[3]), slice(ends[3], ends[4])
    lax.fori_loop(0, pairs, partial(attend, [
        (slice(0, ends[3]), third, False, False), (third, slice(0, ends[2]), True, False)]), 0)
    x_moves[2].wait()
    project(3)
    lax.fori_loop(0, pairs, partial(attend, [
        (slice(0, ends[4]), fourth, False, True), (fourth, slice(0, ends[3]), True, True)]), 0)

    def ff_loads(c):
        slot = lax.rem(c, 2)
        cols = pl.ds(pl.multiple_of(c * COLS, COLS), COLS)
        return [
            pltpu.make_async_copy(w_gate.at[:, cols], both_buf.at[slot, :, pl.ds(0, COLS)], ff_sem.at[slot, 0]),
            pltpu.make_async_copy(w_up.at[:, cols], both_buf.at[slot, :, pl.ds(COLS, COLS)], ff_sem.at[slot, 1]),
            pltpu.make_async_copy(w_down.at[cols, :], down_buf.at[slot], ff_sem.at[slot, 2]),
        ]

    for copy in ff_loads(0):
        copy.start()

    loads[3].wait()

    def project_tile(i, _):
        tile = pl.ds(pl.multiple_of(i * positions, positions), positions)
        mixed = o_t[:, tile].T
        value = x_in[tile, :].astype(F32) + dot(mixed, w_out[...])
        normed = (value * inverse_rms(value) * gain_two[...].reshape(1, features)).astype(BF)
        x_one[tile, :] = value
        acc[tile, :] = value
        n2[tile, :] = normed
        n2_t[:, tile] = normed.T
        d_one[tile, :] = jnp.zeros((positions, features), F32)
        return 0

    lax.fori_loop(0, count, project_tile, 0)
    own[2].wait()
    for copy in g_moves:
        copy.wait()

    down = reducer.n + reducer.e + 1
    late_down = out_chunk + 4

    def shrink_plan(u):
        late = u - late_down
        chunk = jnp.where(u < out_chunk, u, jnp.where(u == out_chunk + 1, out_chunk, out_chunk + 1 + late // 4))
        soon = (u >= 0) & ((u < out_chunk) | (u == out_chunk + 1))
        valid = soon | ((late >= 0) & (late <= 4 * (groups - 1)) & (lax.rem(late, 4) == 0))
        return chunk, valid

    def spread_plan(u):
        return shrink_plan(u - GAP * down)

    def advance(u):
        reducer.shrink_round(u, shrink_plan)
        reducer.spread_round(u, spread_plan)

    def put(c, t, piece):
        for half in range(2):
            grads[c, t, half] = piece[:, 128 * half : 128 * half + 128].astype(BF)

    half_tokens = tokens // 2

    def ff_chunk(c, _):
        slot = lax.rem(c, 2)

        @pl.when(c + 1 < ff_chunks)
        def _():
            for copy in ff_loads(c + 1):
                copy.start()

        for copy in ff_loads(c):
            copy.wait()
        for i in range(2):
            tile = slice(half_tokens * i, half_tokens * (i + 1))
            both = dot(n2[tile, :], both_buf[slot])
            gate, up = both[:, :COLS], both[:, COLS:]
            d_hidden = dot(g_in[tile, :], down_buf[slot], NTRANS)
            square = gate * gate
            bend = 0.7978845608028654 * 0.044715
            turn = jnp.tanh(gate * (0.7978845608028654 + bend * square))
            rise = 0.5 + 0.5 * turn
            activated = gate * rise
            slope = rise + 0.5 * gate * (1.0 - turn * turn) * (0.7978845608028654 + 3.0 * bend * square)
            low_h = (activated * up).astype(BF)
            low_both = jnp.concatenate([(d_hidden * up * slope).astype(BF), (d_hidden * activated).astype(BF)], axis=1)
            d_both[tile, :] = low_both
            h_low[tile, :] = low_h
            acc[tile, :] += dot(low_h, down_buf[slot])
            d_one[tile, :] += dot(low_both, both_buf[slot], NTRANS)
        made = dot(n2_t[...], d_both[...])
        put(c, 0, made[:, :COLS])
        put(c, 1, made[:, COLS:])
        made = dot(h_low[...].T, g_in[...])
        for j in range(NT):
            for half in range(2):
                at = COLS * j + 128 * half
                grads[c, 2, half, COLS * j : COLS * (j + 1), :] = made[:, at : at + 128].astype(BF)
        reducer.shrink_round(c, shrink_plan)
        return 0

    lax.fori_loop(0, ff_chunks, ff_chunk, 0)

    gains[...] = jnp.zeros_like(gains)
    for d in range(count):
        tile = tile_of(d)
        sent[tile, :] = acc[tile, :].astype(BF)

    def whole_back(a, dst):
        own_copy = pltpu.make_async_copy(part_of(sent, 0), dst.at[seq], own_sem.at[a])
        return [own_copy] + [to_peer(a, d, part_of(sent, d), dst.at[seq]) for d in range(1, count)]

    def piece_back(a, dst, i, pieces):
        rows = positions // pieces
        for d in range(2, count):
            low = pl.multiple_of(positions * d + i * rows, 16)
            to = pl.ds(pl.multiple_of(i * rows, 16), rows)
            to_peer(a, d, sent.at[pl.ds(low, rows)], dst.at[seq, to]).start()

    y_moves = whole_back(0, y_back)
    for copy in y_moves[:2]:
        copy.start()
    for d in range(count):
        tile = tile_of(d)
        value = x_one[tile, :]
        inverse = inverse_rms(value)
        slope = d_one[tile, :]
        hat = value * inverse
        gains[1:2, :] += jnp.sum(slope * hat, axis=0, keepdims=True)
        weighted = slope * gain_two[...].reshape(1, features)
        pulled = inverse * (weighted - hat * jnp.mean(weighted * hat, axis=-1, keepdims=True))
        total = g_in[tile, :].astype(F32) + pulled
        d_one[tile, :] = total
        low = total.astype(BF)
        g_in[tile, :] = low
        d_mixed = dot(low, w_out[...], NTRANS).astype(BF)
        n2[tile, :] = d_mixed
        n2_t[:, tile] = d_mixed.T
    reducer.shrink_round(jnp.int32(out_chunk), shrink_plan)

    width = 256

    def slope_of(tile, group):
        return sum(dot(made[tile, group], w_qkv[t, :, group], NTRANS) for t, made in enumerate((q, k, v)))

    def backward_pair(step, _):
        g, j = step // 2, lax.rem(step, 2)
        cols = pl.ds(pl.multiple_of(step * 128, 128), 128)
        key_pair, value_pair = k[:, cols], v[:, cols]
        key_t = key_pair.T
        dq = []
        for h in range(2):
            key, value = half_of(key_pair, h), half_of(value_pair, h)
            rows = pl.ds(pl.multiple_of(step * 128 + HEAD_DIM * h, HEAD_DIM), HEAD_DIM)
            dq_parts = []
            for i in range(tokens // width):
                qs = slice(width * i, width * (i + 1))
                scores = scores_of(key, slice(0, tokens), qs, cols)
                prob = jnp.exp2(scores - lse[step * 2 + h, 0:1, qs])
                delta = jnp.sum(n2_t[rows, qs].astype(F32) * o_t[rows, qs].astype(F32), axis=0, keepdims=True)
                d_prob = dot(value, n2[qs, cols], NTRANS)
                d_score = (prob * (d_prob - delta)).astype(BF)
                low = prob.astype(BF)
                dv = dot(low, n2[qs, cols])
                dk = dot(d_score, q[qs, cols])
                if i == 0:
                    dv_acc[h] = dv
                    dk_acc[h] = dk
                else:
                    dv_acc[h] += dv
                    dk_acc[h] += dk
                dq_parts.append((dot(key_t[HEAD_DIM * h : HEAD_DIM * (h + 1)], d_score) * scale).astype(BF))
            dq.append(jnp.concatenate(dq_parts, axis=1))
            if h == 0:

                @pl.when(step == 0)
                def _():
                    for t in range(NT):
                        put(out_chunk, t, dot(o_t[...], g_in[:, COLS * t : COLS * (t + 1)]))

                advance(out_chunk + 1 + 2 * step)

                @pl.when(step < Y_PIECES // 2)
                def _():
                    piece_back(0, y_back, 2 * step, Y_PIECES)
        lane = lax.broadcasted_iota(jnp.int32, (tokens, 128), 1) < HEAD_DIM
        q[:, cols] = jnp.concatenate(dq, axis=0).T
        k[:, cols] = (jnp.where(lane, dk_acc[0], dk_acc[1]) * scale).astype(BF)
        v[:, cols] = jnp.where(lane, dv_acc[0], dv_acc[1]).astype(BF)

        @pl.when(j == 1)
        def _():
            group = pl.ds(pl.multiple_of(g * COLS, COLS), COLS)
            for t, made in enumerate((q, k, v)):
                put(out_chunk + 1 + g, t, dot(n1_t[...], made[:, group]))

        advance(out_chunk + 2 + 2 * step)

        @pl.when(step < Y_PIECES // 2)
        def _():
            piece_back(0, y_back, 2 * step + 1, Y_PIECES)

        @pl.when((j == 1) & (g < groups - 1))
        def _():
            for d in range(count):
                back = slope_of(tile_of(d), pl.ds(pl.multiple_of(g * COLS, COLS), COLS))
                acc[tile_of(d), :] = jnp.where(g == 0, back, acc[tile_of(d), :] + back)

        return 0

    lax.fori_loop(0, pairs, backward_pair, 0)

    for copy in y_moves:
        copy.wait()
    dx_moves = whole_back(1, dx_back)
    for d in reversed(range(count)):
        tile = tile_of(d)
        slope = acc[tile, :] + slope_of(tile, slice(features - COLS, features))
        value = x_in[tile, :].astype(F32)
        inverse = inverse_rms(value)
        hat = value * inverse
        gains[0:1, :] += jnp.sum(slope * hat, axis=0, keepdims=True)
        weighted = slope * gain_one[...].reshape(1, features)
        pulled = inverse * (weighted - hat * jnp.mean(weighted * hat, axis=-1, keepdims=True))
        sent[tile, :] = (d_one[tile, :] + pulled).astype(BF)
    for copy in dx_moves[:2]:
        copy.start()

    axes = links.all()

    def gain_copy(i):
        return pltpu.make_async_remote_copy(
            src_ref=gains, dst_ref=gains_in.at[i], send_sem=gain_send.at[i], recv_sem=gain_recv.at[i],
            device_id=axes[i], device_id_type=MESH)

    begin = out_chunk + 1 + 2 * pairs
    last = late_down + 4 * (groups - 1) + GAP * (down + reducer.n + 1)

    def tail(r, _):
        for i in range(len(axes) + 1):

            @pl.when(r == begin + i)
            def _():
                if i > 0:
                    gain_copy(i - 1).wait()
                    gains[...] += gains_in[i - 1]
                if i < len(axes):
                    gain_copy(i).start()

        advance(r)

        @pl.when(r < begin + X_PIECES)
        def _():
            piece_back(1, dx_back, r - begin, X_PIECES)

        return 0

    lax.fori_loop(begin, max(last + 1, begin + max(len(axes) + 1, X_PIECES)), tail, 0)
    gain_sums[...] = gains[...]
    for copy in dx_moves:
        copy.wait()


def run_layer(row_bits, blocks, ids, cotangent, w_query, w_key, w_value, w_out, gain_one, gain_two, w_gate, w_up, w_down):
    count, positions, features = blocks.shape
    hidden = w_gate.shape[1]
    tokens, heads = count * positions, features // HEAD_DIM
    chunks = hidden // COLS + 1 + features // COLS
    axes = row_bits + 2
    sizes = (tokens, positions, features, hidden, heads)
    anywhere, inside = pl.BlockSpec(memory_space=pl.ANY), pl.BlockSpec(memory_space=pltpu.VMEM)
    back = jax.ShapeDtypeStruct(blocks.shape, BF)
    low = pltpu.VMEM((tokens, features), BF)
    turned = pltpu.VMEM((features, tokens), BF)
    full = pltpu.VMEM((tokens, features), F32)
    dma = pltpu.SemaphoreType.DMA
    return pl.pallas_call(
        partial(layer_kernel, row_bits, sizes),
        out_shape=(back, back, pltpu.VMEM((chunks, NT, 2, PIECE, 128), BF), jax.ShapeDtypeStruct((8, features), F32)),
        in_specs=[anywhere] * 7 + [inside] * 2 + [anywhere] * 3,
        out_specs=[anywhere] * 2 + [inside] * 2,
        scratch_shapes=[
            low, low,
            pltpu.VMEM((count, count, positions), jnp.int32), pltpu.VMEM((8, tokens), jnp.int32), pltpu.VMEM((tokens, 128), jnp.int32),
            turned, low, low, low, turned, pltpu.VMEM((heads, 8, tokens), F32), full, low, turned, full, full, low,
            pltpu.VMEM((tokens, 2 * COLS), BF), pltpu.VMEM((tokens, COLS), BF),
            pltpu.VMEM((3, features, features), BF), pltpu.VMEM((features, features), BF),
            pltpu.VMEM((2, features, 2 * COLS), BF), pltpu.VMEM((2, COLS, features), BF),
            pltpu.VMEM((2, tokens, 128), F32), pltpu.VMEM((2, tokens, 128), F32),
            pltpu.VMEM((8, features), F32), pltpu.VMEM((axes, 8, features), F32),
        ] + reducer_scratch(row_bits) + [
            dma((4,)), dma((2, 3)), dma((3,)), dma((3, count)), dma((3, count)), dma((axes,)), dma((axes,)),
        ],
        compiler_params=pltpu.CompilerParams(collective_id=0, has_side_effects=True, vmem_limit_bytes=49 * 2**20),
        cost_estimate=pl.CostEstimate(flops=60 * 10**9, bytes_accessed=60 * 10**6, transcendentals=10**7),
    )(blocks, ids, cotangent, w_query, w_key, w_value, w_out, gain_one, gain_two, w_gate, w_up, w_down)


def widen_kernel(
    ff_chunks, groups,
    low, y_in, dx_in, gain_sums,
    y, dx, g_q, g_k, g_v, g_out, g_one, g_two, g_gate, g_up, g_down,
    wide, wide_down, held, out_sem, move_sem,
):
    chunks = ff_chunks + 1 + groups
    arrive = [pltpu.make_async_copy(src, held.at[i], move_sem.at[0, i]) for i, src in enumerate((y_in, dx_in))]
    leave = [pltpu.make_async_copy(held.at[i], dst, move_sem.at[1, i]) for i, dst in enumerate((y, dx))]

    def stores(c):
        slot = c % 3
        cols = pl.ds(COLS * c, COLS)
        if c < ff_chunks:
            pairs = [(wide.at[slot, 0], g_gate.at[:, cols]), (wide.at[slot, 1], g_up.at[:, cols]), (wide_down.at[slot], g_down.at[cols, :])]
        elif c == ff_chunks:
            pairs = [(wide.at[slot, t], g_out.at[:, pl.ds(COLS * t, COLS)]) for t in range(NT)]
        else:
            cols = pl.ds(COLS * (c - ff_chunks - 1), COLS)
            pairs = [(wide.at[slot, t], made.at[:, cols]) for t, made in enumerate((g_q, g_k, g_v))]
        return [pltpu.make_async_copy(src, dst, out_sem.at[slot, t]) for t, (src, dst) in enumerate(pairs)]

    for copy in arrive:
        copy.start()
    g_one[...] = gain_sums[0, :]
    g_two[...] = gain_sums[1, :]
    for c in range(chunks):
        if c >= 3:
            for copy in stores(c - 3):
                copy.wait()
        for half in range(2):
            cols = slice(128 * half, 128 * half + 128)
            for t in range(NT):
                if t == 2 and c < ff_chunks:
                    for j in range(NT):
                        at = COLS * j + 128 * half
                        wide_down[c % 3, :, at : at + 128] = low[c, t, half, COLS * j : COLS * (j + 1), :].astype(F32)
                else:
                    wide[c % 3, t, :, cols] = low[c, t, half].astype(F32)
        for copy in stores(c):
            copy.start()
        if c < 2:
            arrive[c].wait()
            leave[c].start()
    for c in range(chunks - 3, chunks):
        for copy in stores(c):
            copy.wait()
    for copy in leave:
        copy.wait()


def widen(summed, y, dx, gains, features, hidden):
    anywhere, inside = pl.BlockSpec(memory_space=pl.ANY), pl.BlockSpec(memory_space=pltpu.VMEM)
    square, gain = jax.ShapeDtypeStruct((features, features), F32), jax.ShapeDtypeStruct((features,), F32)
    flat, tall = jax.ShapeDtypeStruct((features, hidden), F32), jax.ShapeDtypeStruct((hidden, features), F32)
    back = jax.ShapeDtypeStruct(y.shape, y.dtype)
    dma = pltpu.SemaphoreType.DMA
    return pl.pallas_call(
        partial(widen_kernel, hidden // COLS, features // COLS),
        out_shape=(back, back) + (square,) * 4 + (gain,) * 2 + (flat, flat, tall),
        in_specs=[inside] + [pl.BlockSpec(memory_space=pltpu.HBM)] * 2 + [inside],
        out_specs=[anywhere] * 6 + [inside] * 2 + [anywhere] * 3,
        scratch_shapes=[
            pltpu.VMEM((3, NT, PIECE, COLS), F32), pltpu.VMEM((3, COLS, features), F32), pltpu.VMEM((2,) + y.shape, BF),
            dma((3, NT)), dma((2, 2)),
        ],
        compiler_params=pltpu.CompilerParams(vmem_limit_bytes=48 * 2**20),
    )(pltpu.with_memory_space_constraint(summed, pltpu.VMEM), y, dx, gains)


def body(row_bits, blocks, segment_ids, cotangent, w_query, w_key, w_value, w_out, norm_one, norm_two, w_gate, w_up, w_down):
    features, hidden = w_gate.shape
    y, dx, summed, gains = run_layer(
        row_bits, blocks, segment_ids, cotangent, w_query, w_key, w_value, w_out, norm_one, norm_two, w_gate, w_up, w_down)
    return widen(summed, y, dx, gains, features, hidden)


def solution(mesh):
    split = P("rows", "seq", None)
    row_bits = (mesh.shape["rows"] - 1).bit_length()
    return jax.shard_map(
        partial(body, row_bits),
        mesh=mesh,
        in_specs=(split, P("rows", "seq"), split) + (P(),) * 9,
        out_specs=(split, split) + (P(),) * 9,
        check_vma=False,
    )
```

```python
from functools import partial

import jax
import jax.numpy as jnp
from jax import lax
from jax.experimental import pallas as pl
from jax.experimental.pallas import tpu as pltpu
from jax.sharding import PartitionSpec as P

MESH = pl.DeviceIdType.MESH
HEAD_DIM = 64
EPSILON = 1e-06
MASKED = -1000000000.0
PIECE = 768
NT = 3
COLS = 256
SLOTS = 4
GAP = 2
Y_PIECES = 4
X_PIECES = 16
BF = jnp.bfloat16
F32 = jnp.float32
NN = (((1,), (0,)), ((), ()))
NTRANS = (((1,), (1,)), ((), ()))


def dot(left, right, dims=NN):
    return lax.dot_general(left, right, dims, preferred_element_type=F32)


def flip(index, bit):
    unit = 1 << bit
    own = lax.rem(index // unit, 2)
    return own, index + (1 - 2 * own) * unit


class Links:
    def __init__(self, row_bits):
        seq, row = lax.axis_index("seq"), lax.axis_index("rows")
        self.seq, self.row = seq, row
        self.core, other = flip(seq, 0)
        self.other_core = (other, row)
        x_bit, x_other = flip(seq, 1)
        diagonal = flip(other, 1)[1]
        self.peers = [seq, other, x_other, diagonal]
        dims = [(x_bit, (x_other, row))]
        for bit in range(row_bits):
            own, partner = flip(row, bit)
            dims.append((own, (seq, partner)))
        self.halving = dims[:3]
        self.extra = dims[3:]
        n = len(self.halving)
        orders = [(0, 1, 2), (1, 2, 0), (2, 0, 1)]
        others = [(1, 0, 2), (1, 2, 0), (2, 0, 1)]
        self.orders = [[[d for d in order if d < n] for order in both] for both in (orders, others)]

    def level(self, c, t, k):
        here, there = (both[t][k] for both in self.orders)
        if here == there:
            return self.halving[here]
        even = 1 - lax.rem(c, 2)
        (own_a, (seq_a, row_a)), (own_b, (seq_b, row_b)) = self.halving[here], self.halving[there]
        pick = lambda a, b: a + (b - a) * even
        return pick(own_a, own_b), (pick(seq_a, seq_b), pick(row_a, row_b))

    def all(self):
        return [self.other_core] + [p for _, p in self.halving + self.extra]

    def greet(self):
        barrier = pltpu.get_barrier_semaphore()
        whom = self.all() + [(self.peers[3], self.row)]
        for partner in whom:
            pl.semaphore_signal(barrier, inc=1, device_id=partner, device_id_type=MESH)
        pl.semaphore_wait(barrier, len(whom))


class Reducer:
    def __init__(self, links, grads, landing, small, send, recv, free):
        self.l, self.g, self.landing, self.small = links, grads, landing, small
        self.send, self.recv, self.free = send, recv, free
        n, e = len(links.halving), len(links.extra)
        self.n, self.e = n, e

    def span(self, c, t, level):
        low = 0
        for k in range(level):
            low = low + self.l.level(c, t, k)[0] * (PIECE >> (k + 1))
        return low if level == 0 else pl.multiple_of(low, 16)

    def copies(self, c, stage):
        l, n, e = self.l, self.n, self.e
        core, slot = l.core, lax.rem(c, SLOTS)
        if stage == 0:
            dst = self.landing.at[slot, :, pl.ds(0, PIECE)]
            return [self.make(self.g.at[c, :, 1 - core], dst, c, stage, 0, l.other_core)]
        if stage <= n:
            out = []
            for t in range(NT):
                own, partner = l.level(c, t, stage - 1)
                rows = PIECE >> stage
                low = pl.multiple_of(self.span(c, t, stage - 1) + (1 - own) * rows, 16)
                src = self.g.at[c, t, core, pl.ds(low, rows)]
                dst = self.landing.at[slot, t, pl.ds(2 * PIECE - 2 * rows, rows)]
                out.append(self.make(src, dst, c, stage, t, partner))
            return out
        rows = PIECE >> n
        if stage <= n + e:
            partner = l.extra[stage - n - 1][1]
            out = []
            for t in range(NT):
                src = self.g.at[c, t, core, pl.ds(self.span(c, t, n), rows)]
                out.append(self.make(src, self.small.at[slot, stage - n - 1, t], c, stage, t, partner))
            return out
        k = 2 * n + e + 1 - stage
        if k > 0:
            out = []
            for t in range(NT):
                view = self.g.at[c, t, core, pl.ds(self.span(c, t, k), PIECE >> k)]
                out.append(self.make(view, view, c, stage, t, l.level(c, t, k - 1)[1]))
            return out
        view = self.g.at[c, :, core]
        return [self.make(view, view, c, stage, 0, l.other_core)]

    def make(self, src, dst, c, stage, t, partner):
        slot = lax.rem(c, SLOTS)
        return pltpu.make_async_remote_copy(
            src_ref=src, dst_ref=dst, send_sem=self.send.at[slot, stage, t], recv_sem=self.recv.at[slot, stage, t],
            device_id=partner, device_id_type=MESH)

    def fold(self, c, stage):
        n, e = self.n, self.e
        if stage > n + e:
            return
        core, slot = self.l.core, lax.rem(c, SLOTS)
        rows = PIECE >> min(stage, n)
        for t in range(NT):
            view = self.g.at[c, t, core, pl.ds(self.span(c, t, min(stage, n)), rows)]
            if stage <= n:
                got = self.landing[slot, t, pl.ds(0 if stage == 0 else 2 * PIECE - 2 * rows, rows)]
            else:
                got = self.small[slot, stage - n - 1, t]
            view[...] = view[...] + got

    def partners(self, c, level):
        if level == 0:
            return [(0, self.l.other_core)]
        return [(t, self.l.level(c, t, level - 1)[1]) for t in range(NT)]

    def shrink(self, k, c):
        if k > 0:
            for copy in self.copies(c, k - 1):
                copy.wait()
            self.fold(c, k - 1)
            if k - 1 <= self.n:
                for t, partner in self.partners(c, k - 1):
                    pl.semaphore_signal(self.free.at[k - 1, t, lax.rem(c, 2)], inc=1, device_id=partner, device_id_type=MESH)
        if k <= self.n + self.e:
            for copy in self.copies(c, k):
                copy.start()

    def spread(self, j, c):
        stage = self.n + self.e + 1 + j
        if j > 0:
            for copy in self.copies(c, stage - 1):
                copy.wait()
        if j <= self.n:
            for t, _ in self.partners(c, self.n - j):
                pl.semaphore_wait(self.free.at[self.n - j, t, lax.rem(c, 2)], 1)
            for copy in self.copies(c, stage):
                copy.start()

    def shrink_round(self, u, plan):
        for k in reversed(range(self.n + self.e + 2)):
            c, valid = plan(u - GAP * k)
            pl.when(valid)(partial(self.shrink, k, c))

    def spread_round(self, u, plan):
        for j in reversed(range(self.n + 2)):
            c, valid = plan(u - GAP * j)
            pl.when(valid)(partial(self.spread, j, c))


def reducer_scratch(row_bits):
    n, e = min(3, row_bits + 1), max(0, row_bits - 2)
    stages = 2 + 2 * n + e
    return [
        pltpu.VMEM((SLOTS, NT, 2 * PIECE - (PIECE >> n), 128), BF),
        pltpu.VMEM((SLOTS, max(e, 1), NT, PIECE >> n, 128), BF),
        pltpu.SemaphoreType.DMA((SLOTS, stages, NT)),
        pltpu.SemaphoreType.DMA((SLOTS, stages, NT)),
        pltpu.SemaphoreType.REGULAR((n + 1, NT, 2)),
    ]


def half_of(pair, which):
    lane = lax.broadcasted_iota(jnp.int32, pair.shape, 1)
    return jnp.where((lane // HEAD_DIM) == which, pair, jnp.zeros_like(pair))


def inverse_rms(value):
    return lax.rsqrt(jnp.mean(value * value, axis=-1, keepdims=True) + EPSILON)


def layer_kernel(
    row_bits, sizes,
    blocks, ids, cotangent, w_q_hbm, w_k_hbm, w_v_hbm, w_out_hbm, gain_one, gain_two, w_gate, w_up, w_down,
    y_back, dx_back, grads, gain_sums,
    x_in, g_in, id_rows, id_q, id_k, n1_t, q, k, v, o_t, lse, x_one, n2, n2_t, acc, d_one, sent, d_both, h_low, w_qkv, w_out, both_buf, down_buf,
    dk_acc, dv_acc, gains, gains_in,
    landing, small, send, recv, free,
    w_sem, ff_sem, own_sem, row_send, row_recv, gain_send, gain_recv,
):
    tokens, positions, features, hidden, heads = sizes
    ff_chunks, groups, pairs = hidden // COLS, features // COLS, heads // 2
    count = tokens // positions
    out_chunk = ff_chunks
    chunks = ff_chunks + 1 + groups
    scale = HEAD_DIM ** (-0.5)
    scale_two = scale * 1.4426950408889634
    links = Links(row_bits)
    seq, row = links.seq, links.row
    reducer = Reducer(links, grads, landing, small, send, recv, free)

    def tile_of(d):
        return slice(positions * d, positions * (d + 1))

    def part_of(ref, d):
        return ref.at[pl.ds(positions * d, positions)]

    loads = [pltpu.make_async_copy(w, w_qkv.at[i], w_sem.at[i]) for i, w in enumerate((w_q_hbm, w_k_hbm, w_v_hbm))]
    loads.append(pltpu.make_async_copy(w_out_hbm, w_out, w_sem.at[3]))
    own = [
        pltpu.make_async_copy(blocks.at[seq], part_of(x_in, 0), own_sem.at[0]),
        pltpu.make_async_copy(ids, id_rows.at[0], own_sem.at[1]),
        pltpu.make_async_copy(cotangent.at[seq], part_of(g_in, 0), own_sem.at[2]),
    ]
    own[0].start()
    for copy in loads:
        copy.start()
    own[1].start()
    own[2].start()
    links.greet()

    def to_peer(a, d, src, dst):
        return pltpu.make_async_remote_copy(
            src_ref=src, dst_ref=dst, send_sem=row_send.at[a, d], recv_sem=row_recv.at[a, d],
            device_id=(links.peers[d], row), device_id_type=MESH)

    x_moves = [to_peer(0, d, blocks.at[links.peers[d]], part_of(x_in, d)) for d in range(1, count)]
    id_moves = [to_peer(1, d, ids, id_rows.at[d]) for d in range(1, count)]
    g_moves = [to_peer(2, d, cotangent.at[links.peers[d]], part_of(g_in, d)) for d in range(1, count)]
    for copy in id_moves + x_moves + g_moves:
        copy.start()

    def project(d):
        tile = tile_of(d)
        value = x_in[tile, :].astype(F32)
        normed = (value * inverse_rms(value) * gain_one[...].reshape(1, features)).astype(BF)
        n1_t[:, tile] = normed.T
        for i, made in enumerate((q, k, v)):
            made[tile, :] = dot(normed, w_qkv[i]).astype(BF)

    own[0].wait()
    for copy in loads[:3]:
        copy.wait()
    project(0)
    x_moves[0].wait()
    project(1)

    own[1].wait()
    for copy in id_moves:
        copy.wait()
    for d in range(count):
        id_q[0:1, tile_of(d)] = id_rows[d, pl.ds(seq, 1), :]
    for j in range(tokens // 128):
        block = jnp.broadcast_to(id_q[0:1, 128 * j : 128 * j + 128], (128, 128))
        id_k[128 * j : 128 * j + 128, :] = block.T

    def scores_of(key, keys, queries, cols):
        width = queries.stop - queries.start
        scores = dot(key, q[queries, cols], NTRANS) * scale_two
        same = jnp.concatenate([id_k[keys, :]] * (width // 128), axis=1) == id_q[0:1, queries]
        return jnp.where(same, scores, MASKED)

    o_part = d_one

    def attend(blocks, p, _):
        cols = pl.ds(pl.multiple_of(p * 128, 128), 128)
        used = slice(0, max(keys.stop for keys, _, _, _ in blocks))
        key_pair = k[used, cols]
        value_t = v[used, cols].T
        sides = [half_of(key_pair, h) for h in range(2)]
        work = [(h,) + block for block in blocks for h in range(2)]

        def score(h, keys, queries, joined, final):
            return scores_of(sides[h][keys], keys, queries, cols)

        def weigh(scores, h, keys, queries, joined, final):
            at = p * 2 + h
            largest = jnp.max(scores, axis=0, keepdims=True)
            kept = None
            if joined:
                before = lse[at, 0:1, queries]
                largest = jnp.maximum(before, largest)
                kept = jnp.exp2(before - largest)
            exponent = jnp.exp2(scores - largest)
            total = jnp.sum(exponent, axis=0, keepdims=True)
            if joined:
                total += lse[at, 1:2, queries] * kept
            if final:
                lse[at, 0:1, queries] = largest + jnp.log2(total)
            else:
                lse[at, 0:1, queries] = largest
                lse[at, 1:2, queries] = total
            return exponent.astype(BF), total, kept

        def mix(weights, h, keys, queries, joined, final):
            exponent, total, kept = weights
            rows = pl.ds(pl.multiple_of(p * 128 + HEAD_DIM * h, HEAD_DIM), HEAD_DIM)
            mixed = dot(value_t[HEAD_DIM * h : HEAD_DIM * (h + 1), keys], exponent)
            if joined:
                mixed += o_part[rows, queries] * kept
            if final:
                o_t[rows, queries] = (mixed / total).astype(BF)
            else:
                o_part[rows, queries] = mixed

        scores, behind = score(*work[0]), None
        for i, block in enumerate(work):
            ahead = score(*work[i + 1]) if i + 1 < len(work) else None
            weights = weigh(scores, *block)
            if behind is not None:
                mix(behind[0], *behind[1])
            scores, behind = ahead, (weights, block)
        mix(behind[0], *behind[1])
        return 0

    ends = [positions * d for d in range(count + 1)]
    lax.fori_loop(0, pairs, partial(attend, [(slice(0, ends[2]), slice(0, ends[2]), False, False)]), 0)
    x_moves[1].wait()
    project(2)
    third, fourth = slice(ends[2], ends[3]), slice(ends[3], ends[4])
    lax.fori_loop(0, pairs, partial(attend, [
        (slice(0, ends[3]), third, False, False), (third, slice(0, ends[2]), True, False)]), 0)
    x_moves[2].wait()
    project(3)
    lax.fori_loop(0, pairs, partial(attend, [
        (slice(0, ends[4]), fourth, False, True), (fourth, slice(0, ends[3]), True, True)]), 0)

    def ff_loads(c):
        slot = lax.rem(c, 2)
        cols = pl.ds(pl.multiple_of(c * COLS, COLS), COLS)
        return [
            pltpu.make_async_copy(w_gate.at[:, cols], both_buf.at[slot, :, pl.ds(0, COLS)], ff_sem.at[slot, 0]),
            pltpu.make_async_copy(w_up.at[:, cols], both_buf.at[slot, :, pl.ds(COLS, COLS)], ff_sem.at[slot, 1]),
            pltpu.make_async_copy(w_down.at[cols, :], down_buf.at[slot], ff_sem.at[slot, 2]),
        ]

    for copy in ff_loads(0):
        copy.start()

    loads[3].wait()

    def project_tile(i, _):
        tile = pl.ds(pl.multiple_of(i * positions, positions), positions)
        mixed = o_t[:, tile].T
        value = x_in[tile, :].astype(F32) + dot(mixed, w_out[...])
        normed = (value * inverse_rms(value) * gain_two[...].reshape(1, features)).astype(BF)
        x_one[tile, :] = value
        acc[tile, :] = value
        n2[tile, :] = normed
        n2_t[:, tile] = normed.T
        d_one[tile, :] = jnp.zeros((positions, features), F32)
        return 0

    lax.fori_loop(0, count, project_tile, 0)
    own[2].wait()
    for copy in g_moves:
        copy.wait()

    down = reducer.n + reducer.e + 1
    late_down = out_chunk + 4

    def shrink_plan(u):
        late = u - late_down
        chunk = jnp.where(u < out_chunk, u, jnp.where(u == out_chunk + 1, out_chunk, out_chunk + 1 + late // 4))
        soon = (u >= 0) & ((u < out_chunk) | (u == out_chunk + 1))
        valid = soon | ((late >= 0) & (late <= 4 * (groups - 1)) & (lax.rem(late, 4) == 0))
        return chunk, valid

    def spread_plan(u):
        return shrink_plan(u - GAP * down)

    def advance(u):
        reducer.shrink_round(u, shrink_plan)
        reducer.spread_round(u, spread_plan)

    def put(c, t, piece):
        for half in range(2):
            grads[c, t, half] = piece[:, 128 * half : 128 * half + 128].astype(BF)

    half_tokens = tokens // 2

    def ff_chunk(c, _):
        slot = lax.rem(c, 2)

        @pl.when(c + 1 < ff_chunks)
        def _():
            for copy in ff_loads(c + 1):
                copy.start()

        for copy in ff_loads(c):
            copy.wait()
        for i in range(2):
            tile = slice(half_tokens * i, half_tokens * (i + 1))
            both = dot(n2[tile, :], both_buf[slot])
            gate, up = both[:, :COLS], both[:, COLS:]
            d_hidden = dot(g_in[tile, :], down_buf[slot], NTRANS)
            square = gate * gate
            bend = 0.7978845608028654 * 0.044715
            turn = jnp.tanh(gate * (0.7978845608028654 + bend * square))
            rise = 0.5 + 0.5 * turn
            activated = gate * rise
            slope = rise + 0.5 * gate * (1.0 - turn * turn) * (0.7978845608028654 + 3.0 * bend * square)
            low_h = (activated * up).astype(BF)
            low_both = jnp.concatenate([(d_hidden * up * slope).astype(BF), (d_hidden * activated).astype(BF)], axis=1)
            d_both[tile, :] = low_both
            h_low[tile, :] = low_h
            acc[tile, :] += dot(low_h, down_buf[slot])
            d_one[tile, :] += dot(low_both, both_buf[slot], NTRANS)
        made = dot(n2_t[...], d_both[...])
        put(c, 0, made[:, :COLS])
        put(c, 1, made[:, COLS:])
        made = dot(h_low[...].T, g_in[...])
        for j in range(NT):
            for half in range(2):
                at = COLS * j + 128 * half
                grads[c, 2, half, COLS * j : COLS * (j + 1), :] = made[:, at : at + 128].astype(BF)
        reducer.shrink_round(c, shrink_plan)
        return 0

    lax.fori_loop(0, ff_chunks, ff_chunk, 0)

    gains[...] = jnp.zeros_like(gains)
    for d in range(count):
        tile = tile_of(d)
        sent[tile, :] = acc[tile, :].astype(BF)

    def whole_back(a, dst):
        own_copy = pltpu.make_async_copy(part_of(sent, 0), dst.at[seq], own_sem.at[a])
        return [own_copy] + [to_peer(a, d, part_of(sent, d), dst.at[seq]) for d in range(1, count)]

    def piece_back(a, dst, i, pieces):
        rows = positions // pieces
        for d in range(2, count):
            low = pl.multiple_of(positions * d + i * rows, 16)
            to = pl.ds(pl.multiple_of(i * rows, 16), rows)
            to_peer(a, d, sent.at[pl.ds(low, rows)], dst.at[seq, to]).start()

    y_moves = whole_back(0, y_back)
    for copy in y_moves[:2]:
        copy.start()
    for d in range(count):
        tile = tile_of(d)
        value = x_one[tile, :]
        inverse = inverse_rms(value)
        slope = d_one[tile, :]
        hat = value * inverse
        gains[1:2, :] += jnp.sum(slope * hat, axis=0, keepdims=True)
        weighted = slope * gain_two[...].reshape(1, features)
        pulled = inverse * (weighted - hat * jnp.mean(weighted * hat, axis=-1, keepdims=True))
        total = g_in[tile, :].astype(F32) + pulled
        d_one[tile, :] = total
        low = total.astype(BF)
        g_in[tile, :] = low
        d_mixed = dot(low, w_out[...], NTRANS).astype(BF)
        n2[tile, :] = d_mixed
        n2_t[:, tile] = d_mixed.T
    reducer.shrink_round(jnp.int32(out_chunk), shrink_plan)

    width = 256

    def slope_of(tile, group):
        return sum(dot(made[tile, group], w_qkv[t, :, group], NTRANS) for t, made in enumerate((q, k, v)))

    def backward_pair(step, _):
        g, j = step // 2, lax.rem(step, 2)
        cols = pl.ds(pl.multiple_of(step * 128, 128), 128)
        key_pair, value_pair = k[:, cols], v[:, cols]
        key_t = key_pair.T
        dq = []
        for h in range(2):
            key, value = half_of(key_pair, h), half_of(value_pair, h)
            rows = pl.ds(pl.multiple_of(step * 128 + HEAD_DIM * h, HEAD_DIM), HEAD_DIM)
            dq_parts = []
            for i in range(tokens // width):
                qs = slice(width * i, width * (i + 1))
                scores = scores_of(key, slice(0, tokens), qs, cols)
                prob = jnp.exp2(scores - lse[step * 2 + h, 0:1, qs])
                delta = jnp.sum(n2_t[rows, qs].astype(F32) * o_t[rows, qs].astype(F32), axis=0, keepdims=True)
                d_prob = dot(value, n2[qs, cols], NTRANS)
                d_score = (prob * (d_prob - delta)).astype(BF)
                low = prob.astype(BF)
                dv = dot(low, n2[qs, cols])
                dk = dot(d_score, q[qs, cols])
                if i == 0:
                    dv_acc[h] = dv
                    dk_acc[h] = dk
                else:
                    dv_acc[h] += dv
                    dk_acc[h] += dk
                dq_parts.append((dot(key_t[HEAD_DIM * h : HEAD_DIM * (h + 1)], d_score) * scale).astype(BF))
            dq.append(jnp.concatenate(dq_parts, axis=1))
            if h == 0:

                @pl.when(step == 0)
                def _():
                    for t in range(NT):
                        put(out_chunk, t, dot(o_t[...], g_in[:, COLS * t : COLS * (t + 1)]))

                advance(out_chunk + 1 + 2 * step)

                @pl.when(step < Y_PIECES // 2)
                def _():
                    piece_back(0, y_back, 2 * step, Y_PIECES)
        lane = lax.broadcasted_iota(jnp.int32, (tokens, 128), 1) < HEAD_DIM
        q[:, cols] = jnp.concatenate(dq, axis=0).T
        k[:, cols] = (jnp.where(lane, dk_acc[0], dk_acc[1]) * scale).astype(BF)
        v[:, cols] = jnp.where(lane, dv_acc[0], dv_acc[1]).astype(BF)

        @pl.when(j == 1)
        def _():
            group = pl.ds(pl.multiple_of(g * COLS, COLS), COLS)
            for t, made in enumerate((q, k, v)):
                put(out_chunk + 1 + g, t, dot(n1_t[...], made[:, group]))

        advance(out_chunk + 2 + 2 * step)

        @pl.when(step < Y_PIECES // 2)
        def _():
            piece_back(0, y_back, 2 * step + 1, Y_PIECES)

        @pl.when((j == 1) & (g < groups - 1))
        def _():
            for d in range(count):
                back = slope_of(tile_of(d), pl.ds(pl.multiple_of(g * COLS, COLS), COLS))
                acc[tile_of(d), :] = jnp.where(g == 0, back, acc[tile_of(d), :] + back)

        return 0

    lax.fori_loop(0, pairs, backward_pair, 0)

    for copy in y_moves:
        copy.wait()
    dx_moves = whole_back(1, dx_back)
    for d in reversed(range(count)):
        tile = tile_of(d)
        slope = acc[tile, :] + slope_of(tile, slice(features - COLS, features))
        value = x_in[tile, :].astype(F32)
        inverse = inverse_rms(value)
        hat = value * inverse
        gains[0:1, :] += jnp.sum(slope * hat, axis=0, keepdims=True)
        weighted = slope * gain_one[...].reshape(1, features)
        pulled = inverse * (weighted - hat * jnp.mean(weighted * hat, axis=-1, keepdims=True))
        sent[tile, :] = (d_one[tile, :] + pulled).astype(BF)
    for copy in dx_moves[:2]:
        copy.start()

    axes = links.all()

    def gain_copy(i):
        return pltpu.make_async_remote_copy(
            src_ref=gains, dst_ref=gains_in.at[i], send_sem=gain_send.at[i], recv_sem=gain_recv.at[i],
            device_id=axes[i], device_id_type=MESH)

    begin = out_chunk + 1 + 2 * pairs
    last = late_down + 4 * (groups - 1) + GAP * (down + reducer.n + 1)

    def tail(r, _):
        for i in range(len(axes) + 1):

            @pl.when(r == begin + i)
            def _():
                if i > 0:
                    gain_copy(i - 1).wait()
                    gains[...] += gains_in[i - 1]
                if i < len(axes):
                    gain_copy(i).start()

        advance(r)

        @pl.when(r < begin + X_PIECES)
        def _():
            piece_back(1, dx_back, r - begin, X_PIECES)

        return 0

    lax.fori_loop(begin, max(last + 1, begin + max(len(axes) + 1, X_PIECES)), tail, 0)
    gain_sums[...] = gains[...]
    for copy in dx_moves:
        copy.wait()


def run_layer(row_bits, blocks, ids, cotangent, w_query, w_key, w_value, w_out, gain_one, gain_two, w_gate, w_up, w_down):
    count, positions, features = blocks.shape
    hidden = w_gate.shape[1]
    tokens, heads = count * positions, features // HEAD_DIM
    chunks = hidden // COLS + 1 + features // COLS
    axes = row_bits + 2
    sizes = (tokens, positions, features, hidden, heads)
    anywhere, inside = pl.BlockSpec(memory_space=pl.ANY), pl.BlockSpec(memory_space=pltpu.VMEM)
    back = jax.ShapeDtypeStruct(blocks.shape, BF)
    low = pltpu.VMEM((tokens, features), BF)
    turned = pltpu.VMEM((features, tokens), BF)
    full = pltpu.VMEM((tokens, features), F32)
    dma = pltpu.SemaphoreType.DMA
    return pl.pallas_call(
        partial(layer_kernel, row_bits, sizes),
        out_shape=(back, back, pltpu.VMEM((chunks, NT, 2, PIECE, 128), BF), jax.ShapeDtypeStruct((8, features), F32)),
        in_specs=[anywhere] * 7 + [inside] * 2 + [anywhere] * 3,
        out_specs=[anywhere] * 2 + [inside] * 2,
        scratch_shapes=[
            low, low,
            pltpu.VMEM((count, count, positions), jnp.int32), pltpu.VMEM((8, tokens), jnp.int32), pltpu.VMEM((tokens, 128), jnp.int32),
            turned, low, low, low, turned, pltpu.VMEM((heads, 8, tokens), F32), full, low, turned, full, full, low,
            pltpu.VMEM((tokens, 2 * COLS), BF), pltpu.VMEM((tokens, COLS), BF),
            pltpu.VMEM((3, features, features), BF), pltpu.VMEM((features, features), BF),
            pltpu.VMEM((2, features, 2 * COLS), BF), pltpu.VMEM((2, COLS, features), BF),
            pltpu.VMEM((2, tokens, 128), F32), pltpu.VMEM((2, tokens, 128), F32),
            pltpu.VMEM((8, features), F32), pltpu.VMEM((axes, 8, features), F32),
        ] + reducer_scratch(row_bits) + [
            dma((4,)), dma((2, 3)), dma((3,)), dma((3, count)), dma((3, count)), dma((axes,)), dma((axes,)),
        ],
        compiler_params=pltpu.CompilerParams(collective_id=0, has_side_effects=True, vmem_limit_bytes=49 * 2**20),
        cost_estimate=pl.CostEstimate(flops=60 * 10**9, bytes_accessed=60 * 10**6, transcendentals=10**7),
    )(blocks, ids, cotangent, w_query, w_key, w_value, w_out, gain_one, gain_two, w_gate, w_up, w_down)


def widen_kernel(
    ff_chunks, groups,
    low, y_in, dx_in, gain_sums,
    y, dx, g_q, g_k, g_v, g_out, g_one, g_two, g_gate, g_up, g_down,
    wide, wide_down, held, out_sem, move_sem,
):
    chunks = ff_chunks + 1 + groups
    arrive = [pltpu.make_async_copy(src, held.at[i], move_sem.at[0, i]) for i, src in enumerate((y_in, dx_in))]
    leave = [pltpu.make_async_copy(held.at[i], dst, move_sem.at[1, i]) for i, dst in enumerate((y, dx))]

    def stores(c):
        slot = c % 3
        cols = pl.ds(COLS * c, COLS)
        if c < ff_chunks:
            pairs = [(wide.at[slot, 0], g_gate.at[:, cols]), (wide.at[slot, 1], g_up.at[:, cols]), (wide_down.at[slot], g_down.at[cols, :])]
        elif c == ff_chunks:
            pairs = [(wide.at[slot, t], g_out.at[:, pl.ds(COLS * t, COLS)]) for t in range(NT)]
        else:
            cols = pl.ds(COLS * (c - ff_chunks - 1), COLS)
            pairs = [(wide.at[slot, t], made.at[:, cols]) for t, made in enumerate((g_q, g_k, g_v))]
        return [pltpu.make_async_copy(src, dst, out_sem.at[slot, t]) for t, (src, dst) in enumerate(pairs)]

    for copy in arrive:
        copy.start()
    g_one[...] = gain_sums[0, :]
    g_two[...] = gain_sums[1, :]
    for c in range(chunks):
        if c >= 3:
            for copy in stores(c - 3):
                copy.wait()
        for half in range(2):
            cols = slice(128 * half, 128 * half + 128)
            for t in range(NT):
                if t == 2 and c < ff_chunks:
                    for j in range(NT):
                        at = COLS * j + 128 * half
                        wide_down[c % 3, :, at : at + 128] = low[c, t, half, COLS * j : COLS * (j + 1), :].astype(F32)
                else:
                    wide[c % 3, t, :, cols] = low[c, t, half].astype(F32)
        for copy in stores(c):
            copy.start()
        if c < 2:
            arrive[c].wait()
            leave[c].start()
    for c in range(chunks - 3, chunks):
        for copy in stores(c):
            copy.wait()
    for copy in leave:
        copy.wait()


def widen(summed, y, dx, gains, features, hidden):
    anywhere, inside = pl.BlockSpec(memory_space=pl.ANY), pl.BlockSpec(memory_space=pltpu.VMEM)
    square, gain = jax.ShapeDtypeStruct((features, features), F32), jax.ShapeDtypeStruct((features,), F32)
    flat, tall = jax.ShapeDtypeStruct((features, hidden), F32), jax.ShapeDtypeStruct((hidden, features), F32)
    back = jax.ShapeDtypeStruct(y.shape, y.dtype)
    dma = pltpu.SemaphoreType.DMA
    return pl.pallas_call(
        partial(widen_kernel, hidden // COLS, features // COLS),
        out_shape=(back, back) + (square,) * 4 + (gain,) * 2 + (flat, flat, tall),
        in_specs=[inside] + [pl.BlockSpec(memory_space=pltpu.HBM)] * 2 + [inside],
        out_specs=[anywhere] * 6 + [inside] * 2 + [anywhere] * 3,
        scratch_shapes=[
            pltpu.VMEM((3, NT, PIECE, COLS), F32), pltpu.VMEM((3, COLS, features), F32), pltpu.VMEM((2,) + y.shape, BF),
            dma((3, NT)), dma((2, 2)),
        ],
        compiler_params=pltpu.CompilerParams(vmem_limit_bytes=48 * 2**20),
    )(pltpu.with_memory_space_constraint(summed, pltpu.VMEM), y, dx, gains)


def body(row_bits, blocks, segment_ids, cotangent, w_query, w_key, w_value, w_out, norm_one, norm_two, w_gate, w_up, w_down):
    features, hidden = w_gate.shape
    y, dx, summed, gains = run_layer(
        row_bits, blocks, segment_ids, cotangent, w_query, w_key, w_value, w_out, norm_one, norm_two, w_gate, w_up, w_down)
    return widen(summed, y, dx, gains, features, hidden)


def solution(mesh):
    split = P("rows", "seq", None)
    row_bits = (mesh.shape["rows"] - 1).bit_length()
    return jax.shard_map(
        partial(body, row_bits),
        mesh=mesh,
        in_specs=(split, P("rows", "seq"), split) + (P(),) * 9,
        out_specs=(split, split) + (P(),) * 9,
        check_vma=False,
    )
```
